32 devices in a mesh: fsdp: 8 (over z, x), tp: 4 (over y, core).
Axes of the slice: x: 2, y: 2, z: 4, core: 2. Of those that a mesh axis runs over, the one named last changes fastest.
Arguments:
- master: float32 [14336, 4096], P(('fsdp', 'tp')), may hold values from -0.046875 to 0.046875
- moment_one: float32 [14336, 4096], P(('fsdp', 'tp')), may hold values from -6 to 6
- moment_two: float32 [14336, 4096], P(('fsdp', 'tp')), may hold values from 0.1 to 10
- gradient: bfloat16 [14336, 4096], P(('fsdp', 'tp')), may hold values from -6 to 6
- hidden_act: bfloat16 [4096, 14336], P('fsdp', 'tp'), may hold values from -6 to 6
Outputs:
- new_master: float32 [14336, 4096], P(('fsdp', 'tp'))
- new_one: float32 [14336, 4096], P(('fsdp', 'tp'))
- new_two: float32 [14336, 4096], P(('fsdp', 'tp'))
- decoded: bfloat16 [4096, 4096], P('fsdp', 'tp')
The draws below stay inside these ranges and needn't reach their ends.
All inputs are finite; a program needn't handle non-finite values.
Results may differ from the reference program's by a relative error of at most 0.0049.
Values may be sent and summed in bfloat16 or wider, within the bound.
No kernel may reach another device: no remote copies, remote signals or barrier semaphores. Data moves between devices by JAX's collectives and lax.ppermute only.
A program may use at most 192 MiB of HBM per device.

```python
import math
import jax
import jax.numpy as jnp

D = 4096
FF = 14336
ROWS = 4096


def block_levels(rng, extent, shards, smallest, top_value):
    def one(dim, parts):
        heights = jax.random.uniform(jax.random.fold_in(jax.random.fold_in(rng, 6), dim), (parts,), jnp.float32, smallest / len(shards), top_value / len(shards))
        return jnp.repeat(jnp.exp(heights), extent[dim] // parts).reshape((-1,) + (1,) * (len(extent) - dim - 1))

    loudness = one(*shards[0])
    for cut in shards[1:]:
        loudness = loudness * one(*cut)
    return loudness


def centred(own_key, shape, deviation, bound, shards=(), held_as=jnp.bfloat16):
    gain = block_levels(own_key, shape, shards, -0.22, 0.18) if shards else 1.0
    drawn = jax.random.normal(own_key, shape, jnp.float32) * deviation * gain
    return jnp.minimum(jnp.maximum(drawn, -bound), bound).astype(held_as)


def setup_inputs(seed: int = 0) -> dict:
    arg_keys = jax.random.split(jax.random.key(seed), 6)
    master = centred(arg_keys[0], (FF, D), FF ** -0.5, 0.046875, ((0, 32),), jnp.float32)
    moment_one = centred(arg_keys[1], (FF, D), 1.0, 6.0, ((0, 32),), jnp.float32)
    moment_two = jnp.clip(jnp.exp(math.log(10.0) - 4.6051702 * jax.random.uniform(arg_keys[2], (FF, D), jnp.float32) ** block_levels(arg_keys[2], (FF, D), ((0, 32),), -0.2, 0.2)), 0.1, 10.0)
    gradient = centred(arg_keys[3], (FF, D), 1.0, 6.0, ((0, 32),))
    hidden_act = centred(arg_keys[4], (ROWS, FF), 1.0, 6.0, ((0, 8), (1, 4)))
    return dict(master=master, moment_one=moment_one, moment_two=moment_two, gradient=gradient, hidden_act=hidden_act)


def reference(master, moment_one, moment_two, gradient, hidden_act):
    grad_float = gradient.astype(jnp.float32)
    new_one = 0.9 * moment_one + 0.1 * grad_float
    new_two = 0.95 * moment_two + 0.05 * grad_float * grad_float
    new_master = master - 0.001 * new_one / (jnp.sqrt(new_two) + 1e-08)
    rollout_weight = new_master.astype(jnp.bfloat16)
    decoded = jnp.dot(hidden_act, rollout_weight, preferred_element_type=jnp.float32).astype(jnp.bfloat16)
    return (new_master, new_one, new_two, decoded)
```

```python
import jax
import jax.numpy as jnp
from jax import lax
from jax.experimental import pallas as pl
from jax.experimental.pallas import tpu as pltpu
from jax.sharding import PartitionSpec as P

AXES = ("fsdp", "tp")
ROW_CHUNKS = 2
COL_CHUNKS = 4


def adam_kernel(y_ref, master_ref, one_ref, two_ref, grad_ref, new_master_ref, new_one_ref, new_two_ref, *weight_refs):
    grad = grad_ref[...].astype(jnp.float32)
    new_one = 0.9 * one_ref[...] + 0.1 * grad
    new_two = 0.95 * two_ref[...] + 0.05 * grad * grad
    new_master = master_ref[...] - 0.001 * new_one / (jnp.sqrt(new_two) + 1e-08)
    new_one_ref[...] = new_one
    new_two_ref[...] = new_two
    new_master_ref[...] = new_master
    weight = new_master.astype(jnp.bfloat16)
    quarter = weight.shape[1] // 4
    part = quarter // len(weight_refs)

    def put(first):
        for q, ref in enumerate(weight_refs):
            for i, half in enumerate((first, 1 - first)):
                for core in range(2):
                    at = (2 * half + core) * quarter + q * part
                    ref[:, (2 * i + core) * part : (2 * i + core + 1) * part] = weight[:, at : at + part]

    @pl.when(y_ref[0] == 0)
    def _():
        put(0)

    @pl.when(y_ref[0] != 0)
    def _():
        put(1)


def adam(y, master, moment_one, moment_two, gradient):
    rows, cols = master.shape
    step = max(s for s in range(16, 65, 16) if rows % s == 0)
    block = pl.BlockSpec((step, cols), lambda i: (i, 0))
    piece = pl.BlockSpec((step, cols // COL_CHUNKS), lambda i: (i, 0))
    full = jax.ShapeDtypeStruct((rows, cols), jnp.float32)
    out = pl.pallas_call(
        adam_kernel,
        grid=(rows // step,),
        in_specs=[pl.BlockSpec(memory_space=pltpu.SMEM), block, block, block, block],
        out_specs=[block, block, block] + [piece] * COL_CHUNKS,
        out_shape=[full, full, full]
        + [jax.ShapeDtypeStruct((rows, cols // COL_CHUNKS), jnp.bfloat16)] * COL_CHUNKS,
        compiler_params=pltpu.CompilerParams(vmem_limit_bytes=40 * 1024 * 1024),
        cost_estimate=pl.CostEstimate(flops=12 * rows * cols, bytes_accessed=28 * rows * cols, transcendentals=rows * cols),
        name="adam",
    )(y.reshape(1), master, moment_one, moment_two, gradient)
    return out[0], out[1], out[2], out[3:]


def swap_if(flag, low, high):
    return jnp.where(flag, high, low), jnp.where(flag, low, high)


def in_order(parts, index):
    count = len(parts)
    if count == 1:
        return parts
    half = count // 2
    flag = (index & half) != 0
    pairs = [swap_if(flag, a, b) for a, b in zip(parts[:half], parts[half:])]
    return in_order([p[0] for p in pairs], index) + in_order([p[1] for p in pairs], index)


def local(master, moment_one, moment_two, gradient, hidden_act):
    fsdp, tp = lax.axis_size("fsdp"), lax.axis_size("tp")
    xs = fsdp // tp
    f, t = lax.axis_index("fsdp"), lax.axis_index("tp")
    z, x, y, c = f // xs, f % xs, t // 2, t % 2

    def permute(value, to):
        pairs = []
        for zi in range(tp):
            for xi in range(xs):
                for yi in range(2):
                    for ci in range(2):
                        zo, xo, yo, co = to(zi, xi, yi, ci)
                        pairs.append(((zi * xs + xi) * tp + 2 * yi + ci, (zo * xs + xo) * tp + 2 * yo + co))
        return lax.ppermute(value, AXES, pairs)

    new_master, new_one, new_two, weights = adam(y, master, moment_one, moment_two, gradient)

    rows = hidden_act.shape[0]
    depth = hidden_act.shape[1] // 2
    span = depth // xs
    columns = [
        jnp.concatenate([hidden_act[:, (2 * k + s) * span : (2 * k + s + 1) * span] for k in range(xs)], axis=1)
        for s in range(2)
    ]
    own, other = swap_if(y != 0, *columns)
    part_rows = rows // 2 // ROW_CHUNKS
    own = own.reshape(2, ROW_CHUNKS, part_rows, depth)
    other = other.reshape(2, ROW_CHUNKS, part_rows, depth)
    acts = []
    for m in range(ROW_CHUNKS):
        mine = own[:, m]
        theirs = permute(other[:, m], lambda z, x, y, c: (z, x, 1 - y, c))
        got = []
        for a in range(2):
            data = jnp.where(((z // 2) ^ a ^ y) == 0, mine, theirs)
            first, second = swap_if((z % 2) != 0, data[0], data[1])
            for b, piece in enumerate((first, second)):
                got.append(permute(piece, lambda z, x, y, c: (2 * ((z // 2) ^ a) + c, x, y, (z % 2) ^ b)))
        acts.append(jnp.concatenate(got, axis=0))

    tables = []
    for piece in weights:
        parts = [piece] + [permute(piece, lambda z, x, y, c: (z, x ^ d, y, c)) for d in range(1, xs)]
        here = jnp.stack(in_order(parts, x))
        there = permute(here, lambda z, x, y, c: (z, x, y, 1 - c))
        zero, one = swap_if(c != 0, here, there)
        tables.append(jnp.stack([zero, one], axis=1).reshape(depth, piece.shape[1]))

    blocks = [[], []]
    for m in range(ROW_CHUNKS):
        line = [[], []]
        for table in tables:
            total = jnp.dot(acts[m], table, preferred_element_type=jnp.float32)
            half = table.shape[1] // 2
            back = permute(total[:, half:].astype(jnp.bfloat16), lambda z, x, y, c: (z, x, 1 - y, c))
            total = (total[:, :half] + back).reshape(2, 2, part_rows, half)
            keep, send = swap_if((c ^ (z % 2)) != 0, total[:, 0], total[:, 1])
            back = permute(send.astype(jnp.bfloat16), lambda z, x, y, c: (z ^ 1, x, y, c))
            total = keep + back
            back = permute(total[1].astype(jnp.bfloat16), lambda z, x, y, c: (z ^ 2, x, y, c))
            total = (total[0] + back).astype(jnp.bfloat16)
            keep, send = swap_if(c != 0, total[:, : half // 2], total[:, half // 2 :])
            back = permute(send, lambda z, x, y, c: (z, x, y, 1 - c))
            top, bottom = swap_if(c != 0, keep, back)
            line[0].append(top)
            line[1].append(bottom)
        for s in range(2):
            blocks[s].append(jnp.concatenate(line[s], axis=1))
    decoded = jnp.concatenate(blocks[0] + blocks[1], axis=0)
    return (new_master, new_one, new_two, decoded)


def solution(mesh):
    placed = (
        P(("fsdp", "tp"), None),
        P(("fsdp", "tp"), None),
        P(("fsdp", "tp"), None),
        P(("fsdp", "tp"), None),
        P("fsdp", "tp"),
    )
    return jax.shard_map(
        local,
        mesh=mesh,
        in_specs=placed,
        out_specs=(
            P(("fsdp", "tp"), None),
            P(("fsdp", "tp"), None),
            P(("fsdp", "tp"), None),
            P("fsdp", "tp"),
        ),
        check_vma=False,
    )
```

```python
import jax
import jax.numpy as jnp
from jax import lax
from jax.experimental import pallas as pl
from jax.experimental.pallas import tpu as pltpu
from jax.sharding import PartitionSpec as P

AXES = ("fsdp", "tp")
ROW_CHUNKS = 2
COL_CHUNKS = 2


def adam_kernel(where_ref, master_ref, one_ref, two_ref, grad_ref, *refs):
    new_master_ref, new_one_ref, new_two_ref, weight_ref = refs[-4:]
    grad = grad_ref[...].astype(jnp.float32)
    new_one = 0.9 * one_ref[...] + 0.1 * grad
    new_two = 0.95 * two_ref[...] + 0.05 * grad * grad
    new_master = master_ref[...] - 0.001 * new_one / (jnp.sqrt(new_two) + 1e-08)
    new_one_ref[...] = new_one
    new_two_ref[...] = new_two
    new_master_ref[...] = new_master
    weight_ref[...] = new_master.astype(jnp.bfloat16)


def adam(where, q, args, previous):
    rows, cols = args[0].shape
    width = cols // 4 // COL_CHUNKS
    step = max(s for s in range(16, 225, 16) if rows % s == 0)
    block = pl.BlockSpec((step, width), lambda i, j, w: (i, j * COL_CHUNKS + q))
    piece = pl.BlockSpec((step, width), lambda i, j, w: (i, 2 * ((j % 2) ^ w[1]) + ((j // 2) ^ w[0])))
    full = jax.ShapeDtypeStruct((rows, cols), jnp.float32)
    size = rows * cols // COL_CHUNKS
    return pl.pallas_call(
        adam_kernel,
        grid_spec=pltpu.PrefetchScalarGridSpec(
            num_scalar_prefetch=1,
            grid=(rows // step, 4),
            in_specs=[block] * 4 + [pl.BlockSpec(memory_space=pl.ANY)] * len(previous),
            out_specs=[block, block, block, piece],
        ),
        out_shape=[full, full, full, jax.ShapeDtypeStruct((rows, cols // COL_CHUNKS), jnp.bfloat16)],
        input_output_aliases={5 + i: i for i in range(len(previous))},
        compiler_params=pltpu.CompilerParams(vmem_limit_bytes=32 * 1024 * 1024),
        cost_estimate=pl.CostEstimate(flops=size, bytes_accessed=size, transcendentals=0),
        name="adam",
    )(where, *args, *previous)


def swap_if(flag, low, high):
    return jnp.where(flag, high, low), jnp.where(flag, low, high)


def by_distance(parts, index):
    count = len(parts)
    if count == 1:
        return parts
    half = count // 2
    flag = (index & half) != 0
    pairs = [swap_if(flag, a, b) for a, b in zip(parts[:half], parts[half:])]
    return by_distance([p[0] for p in pairs], index) + by_distance([p[1] for p in pairs], index)


def local(master, moment_one, moment_two, gradient, hidden_act):
    fsdp, tp = lax.axis_size("fsdp"), lax.axis_size("tp")
    xs = fsdp // tp
    f, t = lax.axis_index("fsdp"), lax.axis_index("tp")
    z, x, y, c = f // xs, f % xs, t // 2, t % 2

    def permute(value, to):
        pairs = []
        for zi in range(tp):
            for xi in range(xs):
                for yi in range(2):
                    for ci in range(2):
                        zo, xo, yo, co = to(zi, xi, yi, ci)
                        pairs.append(((zi * xs + xi) * tp + 2 * yi + ci, (zo * xs + xo) * tp + 2 * yo + co))
        return lax.ppermute(value, AXES, pairs)

    rows = hidden_act.shape[0]
    depth = hidden_act.shape[1] // 2
    span = depth // xs // 2
    columns = []
    for s in range(2):
        cores = []
        for k in range(2):
            at = [(4 * i + 2 * s + k) * span for i in range(xs)]
            cores += by_distance([hidden_act[:, a : a + span] for a in at], x)
        columns.append(jnp.concatenate(cores, axis=1))
    own, other = swap_if(y != 0, *columns)
    part_rows = rows // ROW_CHUNKS
    acts = []
    for m in range(ROW_CHUNKS):
        mine = own[m * part_rows : (m + 1) * part_rows]
        theirs = permute(other[m * part_rows : (m + 1) * part_rows], lambda z, x, y, c: (z, x, 1 - y, c))
        first, second = swap_if(((z // 2) ^ y) != 0, mine, theirs)
        got = [
            permute(data, lambda z, x, y, c: (2 * ((z // 2) ^ a) + c, x, y, z % 2))
            for a, data in enumerate((first, second))
        ]
        got = jnp.stack(got)
        also = permute(got, lambda z, x, y, c: (z, x, y, 1 - c))
        near, far = swap_if((c ^ (z % 2)) != 0, got, also)
        acts.append(jnp.stack([near, far], axis=1).reshape(4 * part_rows, depth))

    where = jnp.stack([y, c]).astype(jnp.int32)
    updated = []
    tables = []
    for q in range(COL_CHUNKS):
        *updated, piece = adam(where, q, (master, moment_one, moment_two, gradient), updated)
        parts = [piece] + [permute(piece, lambda z, x, y, c: (z, x ^ d, y, c)) for d in range(1, xs)]
        half = piece.shape[1] // 2
        here = jnp.concatenate([p[:, :half] for p in parts], axis=0)
        there = jnp.concatenate([p[:, half:] for p in parts], axis=0)
        there = permute(there, lambda z, x, y, c: (z, x, y, 1 - c))
        zero, one = swap_if(c != 0, here, there)
        tables.append(jnp.concatenate([zero, one], axis=0))

    blocks = []
    for m in range(ROW_CHUNKS):
        line = []
        for table in tables:
            total = jnp.dot(acts[m], table, preferred_element_type=jnp.float32)
            half = table.shape[1] // 2
            back = permute(total[:, half:].astype(jnp.bfloat16), lambda z, x, y, c: (z, x, 1 - y, c))
            total = (total[:, :half] + back).reshape(2, 2, part_rows, half)
            back = permute(total[:, 1].astype(jnp.bfloat16), lambda z, x, y, c: (z ^ 1, x, y, c))
            total = total[:, 0] + back
            back = permute(total[1].astype(jnp.bfloat16), lambda z, x, y, c: (z ^ 2, x, y, c))
            line.append((total[0] + back).astype(jnp.bfloat16))
        blocks.append(jnp.concatenate(line, axis=1))
    decoded = jnp.concatenate(blocks, axis=0)
    return (*updated, decoded)


def solution(mesh):
    placed = (
        P(("fsdp", "tp"), None),
        P(("fsdp", "tp"), None),
        P(("fsdp", "tp"), None),
        P(("fsdp", "tp"), None),
        P("fsdp", "tp"),
    )
    return jax.shard_map(
        local,
        mesh=mesh,
        in_specs=placed,
        out_specs=(
            P(("fsdp", "tp"), None),
            P(("fsdp", "tp"), None),
            P(("fsdp", "tp"), None),
            P("fsdp", "tp"),
        ),
        check_vma=False,
    )
```

```python
import jax
import jax.numpy as jnp
from jax import lax
from jax.experimental import pallas as pl
from jax.experimental.pallas import tpu as pltpu
from jax.sharding import PartitionSpec as P

AXES = ("fsdp", "tp")
ROW_CHUNKS = 2
COL_CHUNKS = 4


def adam_step(master_ref, one_ref, two_ref, grad_ref, new_master_ref, new_one_ref, new_two_ref, weight_ref):
    grad = grad_ref[...].astype(jnp.float32)
    new_one = 0.9 * one_ref[...] + 0.1 * grad
    new_two = 0.95 * two_ref[...] + 0.05 * grad * grad
    new_master = master_ref[...] - 0.001 * new_one / (jnp.sqrt(new_two) + 1e-08)
    new_one_ref[...] = new_one
    new_two_ref[...] = new_two
    new_master_ref[...] = new_master
    weight_ref[...] = new_master.astype(jnp.bfloat16)


def adam(where, chunks, args, previous):
    rows, cols = args[0].shape
    width = cols // 4 // COL_CHUNKS
    step = max(s for s in range(16, 225, 16) if rows % s == 0)
    count = len(chunks)

    def kernel(where_ref, *refs):
        sources = refs[:4]
        targets = refs[-3 - count : -count]
        y, c = where_ref[0], where_ref[1]
        for q, weight_ref in zip(chunks, refs[-count:]):
            block = pl.BlockSpec((step, width), lambda j, i: (i, j * COL_CHUNKS + q))
            piece = pl.BlockSpec((step, width), lambda j, i: (i, 2 * ((j % 2) ^ c) + ((j // 2) ^ y)))
            pltpu.emit_pipeline(
                adam_step,
                grid=(4, rows // step),
                in_specs=[block] * 4,
                out_specs=[block] * 3 + [piece],
            )(*sources, *targets, weight_ref)

    hbm = pl.BlockSpec(memory_space=pltpu.HBM)
    full = jax.ShapeDtypeStruct((rows, cols), jnp.float32)
    size = rows * cols * count // COL_CHUNKS
    out = pl.pallas_call(
        kernel,
        in_specs=[pl.BlockSpec(memory_space=pltpu.SMEM)] + [hbm] * (4 + len(previous)),
        out_specs=[hbm] * (3 + count),
        out_shape=[full] * 3 + [jax.ShapeDtypeStruct((rows, cols // COL_CHUNKS), jnp.bfloat16)] * count,
        input_output_aliases={5 + i: i for i in range(len(previous))},
        compiler_params=pltpu.CompilerParams(vmem_limit_bytes=60 * 1024 * 1024),
        cost_estimate=pl.CostEstimate(flops=12 * size, bytes_accessed=28 * size, transcendentals=size),
        name="adam",
    )(where, *args, *previous)
    return out[:3], out[3:]


def pack(where, act, xs):
    rows, cols = act.shape
    run = cols // xs // 2
    part = rows // ROW_CHUNKS

    def kernel(where_ref, act_ref, *out_refs):
        for y in range(2):
            for x in range(xs):

                @pl.when((where_ref[0] == y) & (where_ref[2] == x))
                def _():
                    for m in range(ROW_CHUNKS):
                        for s in range(2):
                            for d in range(xs):
                                at = (2 * (x ^ d) + (y ^ s)) * run
                                out_refs[2 * m + s][:, d * run : (d + 1) * run] = act_ref[
                                    m * part : (m + 1) * part, at : at + run
                                ]

    out = pl.pallas_call(
        kernel,
        in_specs=[pl.BlockSpec(memory_space=pltpu.SMEM), pl.BlockSpec(memory_space=pltpu.VMEM)],
        out_specs=[pl.BlockSpec(memory_space=pltpu.VMEM)] * (2 * ROW_CHUNKS),
        out_shape=[jax.ShapeDtypeStruct((part, cols // 2), act.dtype)] * (2 * ROW_CHUNKS),
        compiler_params=pltpu.CompilerParams(vmem_limit_bytes=32 * 1024 * 1024),
        cost_estimate=pl.CostEstimate(flops=0, bytes_accessed=4 * rows * cols, transcendentals=0),
        name="pack",
    )(where, act)
    return out[0::2], out[1::2]


def swap_if(flag, low, high):
    return jnp.where(flag, high, low), jnp.where(flag, low, high)


def after(value, *done):
    return lax.optimization_barrier((value, *done))[0]


def local(master, moment_one, moment_two, gradient, hidden_act):
    fsdp, tp = lax.axis_size("fsdp"), lax.axis_size("tp")
    xs = fsdp // tp
    f, t = lax.axis_index("fsdp"), lax.axis_index("tp")
    z, x, y, c = f // xs, f % xs, t // 2, t % 2
    where = jnp.stack([y, c, x]).astype(jnp.int32)

    def permute(value, to):
        pairs = []
        for zi in range(tp):
            for xi in range(xs):
                for yi in range(2):
                    for ci in range(2):
                        zo, xo, yo, co = to(zi, xi, yi, ci)
                        pairs.append(((zi * xs + xi) * tp + 2 * yi + ci, (zo * xs + xo) * tp + 2 * yo + co))
        return lax.ppermute(value, AXES, pairs)

    rows = hidden_act.shape[0]
    part = rows // ROW_CHUNKS
    own, other = pack(where, hidden_act, xs)

    args = (master, moment_one, moment_two, gradient)
    updated, pieces = adam(where, [0], args, [])
    updated, rest = adam(where, list(range(1, COL_CHUNKS)), args, updated)
    tables, crossed = [], []
    for piece in [*pieces, *rest]:
        if crossed:
            piece = after(piece, crossed[-1])
        parts = [piece] + [permute(piece, lambda z, x, y, c: (z, x ^ d, y, c)) for d in range(1, xs)]
        crossed.append(parts[-1])
        half = piece.shape[1] // 2
        here = jnp.stack([p[:, :half] for p in parts])
        there = jnp.stack([p[:, half:] for p in parts])
        there = permute(there, lambda z, x, y, c: (z, x, y, 1 - c))
        tables.append(jnp.stack(swap_if(c != 0, here, there), axis=1).reshape(-1, half))

    acts, theirs, moved = [], [], []
    for m in range(ROW_CHUNKS):
        send = other[m] if m == 0 else after(other[m], theirs[-1])
        theirs.append(permute(send, lambda z, x, y, c: (z, x, 1 - y, c)))
        pair = swap_if(((z // 2) ^ y) != 0, own[m], theirs[m])
        if m:
            pair = after(pair, moved[-1], crossed[2 * m - 1])
        got = [
            permute(data, lambda z, x, y, c: (2 * ((z // 2) ^ a) + c, x, y, z % 2)) for a, data in enumerate(pair)
        ]
        got = jnp.concatenate(got, axis=0)
        moved.append(got)
        acts.append((got, permute(got, lambda z, x, y, c: (z, x, y, 1 - c))))

    flip = (c ^ (z % 2)) != 0
    backs, leaving, result = [], [], []
    for m in range(ROW_CHUNKS):
        line = []
        for table in tables:
            j = len(backs)
            totals = [jnp.dot(a, table, preferred_element_type=jnp.float32) for a in acts[m]]
            half = table.shape[1] // 2
            send = jnp.stack([total[:, half:].astype(jnp.bfloat16) for total in totals])
            if j >= 2:
                send = after(send, backs[j - 2])
            back = permute(send, lambda z, x, y, c: (z, x, 1 - y, c))
            backs.append(back)
            if j >= 1:
                back = after(back, leaving[-1])
            near, far = swap_if(flip, *[total[:, :half] + b for total, b in zip(totals, back)])
            back = permute(far.astype(jnp.bfloat16), lambda z, x, y, c: (z ^ 1, x, y, c))
            near = near + back
            send = near[part:].astype(jnp.bfloat16)
            leaving.append(send)
            back = permute(send, lambda z, x, y, c: (z ^ 2, x, y, c))
            line.append((near[:part] + back).astype(jnp.bfloat16))
        result.append(jnp.concatenate(line, axis=1))
    decoded = jnp.concatenate(result, axis=0)
    return (*updated, decoded)


def solution(mesh):
    placed = (
        P(("fsdp", "tp"), None),
        P(("fsdp", "tp"), None),
        P(("fsdp", "tp"), None),
        P(("fsdp", "tp"), None),
        P("fsdp", "tp"),
    )
    return jax.shard_map(
        local,
        mesh=mesh,
        in_specs=placed,
        out_specs=(
            P(("fsdp", "tp"), None),
            P(("fsdp", "tp"), None),
            P(("fsdp", "tp"), None),
            P("fsdp", "tp"),
        ),
        check_vma=False,
    )
```

```python
import jax
import jax.numpy as jnp
from jax import lax
from jax.experimental import pallas as pl
from jax.experimental.pallas import tpu as pltpu
from jax.sharding import PartitionSpec as P

AXES = ("fsdp", "tp")
ROW_CHUNKS = 2
COL_CHUNKS = 4


def adam(where, chunks, args, previous):
    rows, cols = args[0].shape
    width = cols // 4 // COL_CHUNKS
    step = max(s for s in range(16, 449, 16) if rows % s == 0)
    tiles = rows // step
    count = len(chunks)
    each = 4 * tiles

    def kernel(where_ref, master_ref, one_ref, two_ref, grad_ref, *refs):
        new_master_ref, new_one_ref, new_two_ref = refs[-3 - count : -count]
        grad = grad_ref[...].astype(jnp.float32)
        new_one = 0.9 * one_ref[...] + 0.1 * grad
        new_two = 0.95 * two_ref[...] + 0.05 * grad * grad
        new_master = master_ref[...] - 0.001 * new_one / (jnp.sqrt(new_two) + 1e-08)
        new_one_ref[...] = new_one
        new_two_ref[...] = new_two
        new_master_ref[...] = new_master
        weight = new_master.astype(jnp.bfloat16)
        for k, weight_ref in enumerate(refs[-count:]):

            @pl.when(pl.program_id(0) // each == k)
            def _():
                weight_ref[...] = weight

    def at(i, w):
        j = i % each // tiles
        return i % tiles, j * COL_CHUNKS + chunks[0] + i // each

    def piece_at(k):
        def index(i, w):
            i = jnp.clip(i - k * each, 0, each - 1)
            j = i // tiles
            return i % tiles, 2 * ((j % 2) ^ w[1]) + ((j // 2) ^ w[0])

        return index

    source = pl.BlockSpec((step, width), at)
    target = pl.BlockSpec((step, width), at)
    pieces = [pl.BlockSpec((step, width), piece_at(k)) for k in range(count)]
    full = jax.ShapeDtypeStruct((rows, cols), jnp.float32)
    size = rows * cols * count // COL_CHUNKS
    out = pl.pallas_call(
        kernel,
        grid_spec=pltpu.PrefetchScalarGridSpec(
            num_scalar_prefetch=1,
            grid=(count * each,),
            in_specs=[source] * 4 + [pl.BlockSpec(memory_space=pl.ANY)] * len(previous),
            out_specs=[target] * 3 + pieces,
        ),
        out_shape=[full] * 3 + [jax.ShapeDtypeStruct((rows, cols // COL_CHUNKS), jnp.bfloat16)] * count,
        input_output_aliases={5 + i: i for i in range(len(previous))},
        compiler_params=pltpu.CompilerParams(vmem_limit_bytes=60 * 1024 * 1024),
        cost_estimate=pl.CostEstimate(flops=size, bytes_accessed=size, transcendentals=0),
        name="adam",
    )(where, *args, *previous)
    return out[:3], out[3:]


def pack(where, act, xs):
    rows, cols = act.shape
    run = cols // xs // 2
    part = rows // ROW_CHUNKS

    def kernel(where_ref, act_ref, *out_refs):
        for y in range(2):
            for x in range(xs):

                @pl.when((where_ref[0] == y) & (where_ref[2] == x))
                def _():
                    for m in range(ROW_CHUNKS):
                        for s in range(2):
                            for d in range(xs):
                                at = (2 * (x ^ d) + (y ^ s)) * run
                                out_refs[2 * m + s][:, d * run : (d + 1) * run] = act_ref[
                                    m * part : (m + 1) * part, at : at + run
                                ]

    out = pl.pallas_call(
        kernel,
        in_specs=[pl.BlockSpec(memory_space=pltpu.SMEM), pl.BlockSpec(memory_space=pltpu.VMEM)],
        out_specs=[pl.BlockSpec(memory_space=pltpu.VMEM)] * (2 * ROW_CHUNKS),
        out_shape=[jax.ShapeDtypeStruct((part, cols // 2), act.dtype)] * (2 * ROW_CHUNKS),
        compiler_params=pltpu.CompilerParams(vmem_limit_bytes=32 * 1024 * 1024),
        cost_estimate=pl.CostEstimate(flops=0, bytes_accessed=4 * rows * cols, transcendentals=0),
        name="pack",
    )(where, act)
    return out[0::2], out[1::2]


def swap_if(flag, low, high):
    return jnp.where(flag, high, low), jnp.where(flag, low, high)


def after(value, *done):
    return lax.optimization_barrier((value, *done))[0] if done else value


def local(master, moment_one, moment_two, gradient, hidden_act):
    fsdp, tp = lax.axis_size("fsdp"), lax.axis_size("tp")
    xs = fsdp // tp
    f, t = lax.axis_index("fsdp"), lax.axis_index("tp")
    z, x, y, c = f // xs, f % xs, t // 2, t % 2
    where = jnp.stack([y, c, x]).astype(jnp.int32)

    def permute(value, to):
        pairs = []
        for zi in range(tp):
            for xi in range(xs):
                for yi in range(2):
                    for ci in range(2):
                        zo, xo, yo, co = to(zi, xi, yi, ci)
                        pairs.append(((zi * xs + xi) * tp + 2 * yi + ci, (zo * xs + xo) * tp + 2 * yo + co))
        return lax.ppermute(value, AXES, pairs)

    rows = hidden_act.shape[0]
    part = rows // ROW_CHUNKS
    own, other = pack(where, hidden_act, xs)

    args = (master, moment_one, moment_two, gradient)
    updated, first = adam(where, [0], args, [])
    updated, rest = adam(where, list(range(1, COL_CHUNKS)), args, updated)
    pieces = [*first, *rest]
    flip = (c ^ (z % 2)) != 0
    crossed, tables = [], []
    theirs, moved, acts = [], [], []
    sends, backs, leaving, result = [], [], [], []

    def to_plane(m):
        send = other[m] if m == 0 else after(other[m], theirs[-1])
        theirs.append(permute(send, lambda z, x, y, c: (z, x, 1 - y, c)))
        pair = swap_if(((z // 2) ^ y) != 0, own[m], theirs[m])
        if m:
            pair = after(pair, moved[-1], crossed[1])
        got = [
            permute(data, lambda z, x, y, c: (2 * ((z // 2) ^ a) + c, x, y, z % 2)) for a, data in enumerate(pair)
        ]
        moved.append(got)

    def to_cores(m, *done):
        got = jnp.concatenate(after(moved[m], *done), axis=0)
        moved[m] = got
        acts.append((got, permute(got, lambda z, x, y, c: (z, x, y, 1 - c))))

    def gather(q, *done):
        piece = after(pieces[q], crossed[-1]) if q else pieces[q]
        parts = [piece] + [permute(piece, lambda z, x, y, c: (z, x ^ d, y, c)) for d in range(1, xs)]
        crossed.append(parts[-1])
        half = piece.shape[1] // 2
        parts = after(parts, *done)
        here = jnp.stack([p[:, :half] for p in parts])
        there = jnp.stack([p[:, half:] for p in parts])
        there = permute(there, lambda z, x, y, c: (z, x, y, 1 - c))
        tables.append(jnp.stack(swap_if(c != 0, here, there), axis=1).reshape(-1, half))

    def multiply(m, q):
        table = tables[q]
        half = table.shape[1] // 2
        totals = [jnp.dot(a, table, preferred_element_type=jnp.float32) for a in acts[m]]
        send = jnp.stack([total[:, half:].astype(jnp.bfloat16) for total in totals])
        if len(backs) >= 2:
            send = after(send, backs[-2])
        sends.append(send)
        backs.append(permute(send, lambda z, x, y, c: (z, x, 1 - y, c)))
        return [total[:, :half] for total in totals], len(backs) - 1

    def reduce(totals, j):
        back = after(backs[j], leaving[-1]) if leaving else backs[j]
        near, far = swap_if(flip, *[total + b for total, b in zip(totals, back)])
        back = permute(far.astype(jnp.bfloat16), lambda z, x, y, c: (z ^ 1, x, y, c))
        near = near + back
        send = near[part:].astype(jnp.bfloat16)
        leaving.append(send)
        back = permute(send, lambda z, x, y, c: (z ^ 2, x, y, c))
        result.append((near[:part] + back).astype(jnp.bfloat16))

    gather(0)
    gather(1)
    to_plane(0)
    to_plane(1)
    to_cores(0)
    jobs = [multiply(0, 0), multiply(0, 1)]
    gather(2, sends[0], sends[1])
    gather(3, backs[0])
    jobs.append(multiply(0, 2))
    to_cores(1, backs[1])
    jobs.append(multiply(0, 3))
    jobs += [multiply(1, q) for q in range(COL_CHUNKS)]
    for job in jobs:
        reduce(*job)
    result = [jnp.concatenate(result[i : i + COL_CHUNKS], axis=1) for i in range(0, len(result), COL_CHUNKS)]
    decoded = jnp.concatenate(result, axis=0)
    return (*updated, decoded)


def solution(mesh):
    placed = (
        P(("fsdp", "tp"), None),
        P(("fsdp", "tp"), None),
        P(("fsdp", "tp"), None),
        P(("fsdp", "tp"), None),
        P("fsdp", "tp"),
    )
    return jax.shard_map(
        local,
        mesh=mesh,
        in_specs=placed,
        out_specs=(
            P(("fsdp", "tp"), None),
            P(("fsdp", "tp"), None),
            P(("fsdp", "tp"), None),
            P("fsdp", "tp"),
        ),
        check_vma=False,
    )
```

```python
import jax
import jax.numpy as jnp
from jax import lax
from jax.experimental import pallas as pl
from jax.experimental.pallas import tpu as pltpu
from jax.sharding import PartitionSpec as P

AXES = ("fsdp", "tp")
ROW_CHUNKS = 2
COL_CHUNKS = 4


def adam(where, chunks, args, previous):
    rows, cols = args[0].shape
    width = cols // 4 // COL_CHUNKS
    step = max(s for s in range(16, 449, 16) if rows % s == 0)
    tiles = rows // step
    count = len(chunks)
    each = 4 * tiles

    def kernel(where_ref, master_ref, one_ref, two_ref, grad_ref, *refs):
        new_master_ref, new_one_ref, new_two_ref = refs[-3 - count : -count]
        grad = grad_ref[...].astype(jnp.float32)
        new_one = 0.9 * one_ref[...] + 0.1 * grad
        new_two = 0.95 * two_ref[...] + 0.05 * grad * grad
        new_master = master_ref[...] - 0.001 * new_one / (jnp.sqrt(new_two) + 1e-08)
        new_one_ref[...] = new_one
        new_two_ref[...] = new_two
        new_master_ref[...] = new_master
        weight = new_master.astype(jnp.bfloat16)
        for k, weight_ref in enumerate(refs[-count:]):

            @pl.when(pl.program_id(0) // each == k)
            def _():
                weight_ref[...] = weight

    def at(i, w):
        j = i % each // tiles
        return i % tiles, j * COL_CHUNKS + chunks[0] + i // each

    def piece_at(k):
        def index(i, w):
            i = jnp.clip(i - k * each, 0, each - 1)
            j = i // tiles
            return i % tiles, 2 * ((j % 2) ^ w[1]) + ((j // 2) ^ w[0])

        return index

    source = pl.BlockSpec((step, width), at)
    target = pl.BlockSpec((step, width), at)
    pieces = [pl.BlockSpec((step, width), piece_at(k)) for k in range(count)]
    full = jax.ShapeDtypeStruct((rows, cols), jnp.float32)
    size = rows * cols * count // COL_CHUNKS
    out = pl.pallas_call(
        kernel,
        grid_spec=pltpu.PrefetchScalarGridSpec(
            num_scalar_prefetch=1,
            grid=(count * each,),
            in_specs=[source] * 4 + [pl.BlockSpec(memory_space=pl.ANY)] * len(previous),
            out_specs=[target] * 3 + pieces,
        ),
        out_shape=[full] * 3 + [jax.ShapeDtypeStruct((rows, cols // COL_CHUNKS), jnp.bfloat16)] * count,
        input_output_aliases={5 + i: i for i in range(len(previous))},
        compiler_params=pltpu.CompilerParams(vmem_limit_bytes=60 * 1024 * 1024),
        cost_estimate=pl.CostEstimate(flops=size, bytes_accessed=size, transcendentals=0),
        name="adam",
    )(where, *args, *previous)
    return out[:3], out[3:]


def pack(where, act, xs):
    rows, cols = act.shape
    run = cols // xs // 2
    part = rows // ROW_CHUNKS

    def kernel(where_ref, act_ref, *out_refs):
        for y in range(2):
            for x in range(xs):

                @pl.when((where_ref[0] == y) & (where_ref[2] == x))
                def _():
                    for m in range(ROW_CHUNKS):
                        for s in range(2):
                            for d in range(xs):
                                at = (2 * (x ^ d) + (y ^ s)) * run
                                out_refs[2 * m + s][:, d * run : (d + 1) * run] = act_ref[
                                    m * part : (m + 1) * part, at : at + run
                                ]

    out = pl.pallas_call(
        kernel,
        in_specs=[pl.BlockSpec(memory_space=pltpu.SMEM), pl.BlockSpec(memory_space=pltpu.VMEM)],
        out_specs=[pl.BlockSpec(memory_space=pltpu.VMEM)] * (2 * ROW_CHUNKS),
        out_shape=[jax.ShapeDtypeStruct((part, cols // 2), act.dtype)] * (2 * ROW_CHUNKS),
        compiler_params=pltpu.CompilerParams(vmem_limit_bytes=32 * 1024 * 1024),
        cost_estimate=pl.CostEstimate(flops=0, bytes_accessed=4 * rows * cols, transcendentals=0),
        name="pack",
    )(where, act)
    return out[0::2], out[1::2]


def swap_if(flag, low, high):
    return jnp.where(flag, high, low), jnp.where(flag, low, high)


def after(value, *done):
    return lax.optimization_barrier((value, *done))[0] if done else value


def local(master, moment_one, moment_two, gradient, hidden_act):
    fsdp, tp = lax.axis_size("fsdp"), lax.axis_size("tp")
    xs = fsdp // tp
    f, t = lax.axis_index("fsdp"), lax.axis_index("tp")
    z, x, y, c = f // xs, f % xs, t // 2, t % 2
    where = jnp.stack([y, c, x]).astype(jnp.int32)

    def permute(value, to):
        pairs = []
        for zi in range(tp):
            for xi in range(xs):
                for yi in range(2):
                    for ci in range(2):
                        zo, xo, yo, co = to(zi, xi, yi, ci)
                        pairs.append(((zi * xs + xi) * tp + 2 * yi + ci, (zo * xs + xo) * tp + 2 * yo + co))
        return lax.ppermute(value, AXES, pairs)

    rows = hidden_act.shape[0]
    part = rows // ROW_CHUNKS
    own, other = pack(where, hidden_act, xs)

    args = (master, moment_one, moment_two, gradient)
    updated, pieces = [], []

    def update(q, *done):
        new, (piece,) = adam(after(where, *done), [q], args, updated)
        updated[:] = new
        pieces.append(piece)

    flip = (c ^ (z % 2)) != 0
    crossed, used, tables = [], [], []
    theirs, pairs, moved, acts = [], [], [], []
    sends, backs, leaving, result = [], [], [], []

    def to_plane(m, *done):
        send = after(other[m], theirs[-1]) if m else other[m]
        theirs.append(permute(send, lambda z, x, y, c: (z, x, 1 - y, c)))
        pair = after(swap_if(((z // 2) ^ y) != 0, own[m], theirs[m]), *done)
        pairs.append(pair)
        moved.append(
            [permute(data, lambda z, x, y, c: (2 * ((z // 2) ^ a) + c, x, y, z % 2)) for a, data in enumerate(pair)]
        )

    def to_cores(m, *done):
        got = jnp.concatenate(after(moved[m], *done), axis=0)
        acts.append((got, permute(got, lambda z, x, y, c: (z, x, y, 1 - c))))

    def gather(q, *done):
        piece = after(pieces[q], crossed[-1]) if q else pieces[q]
        parts = [piece] + [permute(piece, lambda z, x, y, c: (z, x ^ d, y, c)) for d in range(1, xs)]
        crossed.append(parts[-1])
        half = piece.shape[1] // 2
        parts = after(parts, *done)
        here = jnp.stack([p[:, :half] for p in parts])
        there = jnp.stack([p[:, half:] for p in parts])
        used.append(there)
        there = permute(there, lambda z, x, y, c: (z, x, y, 1 - c))
        tables.append(jnp.stack(swap_if(c != 0, here, there), axis=1).reshape(-1, half))

    def multiply(m, q):
        table = tables[q]
        half = table.shape[1] // 2
        totals = [jnp.dot(a, table, preferred_element_type=jnp.float32) for a in acts[m]]
        send = jnp.stack([total[:, half:].astype(jnp.bfloat16) for total in totals])
        send = after(send, *sends[-1:], *backs[-2:-1])
        sends.append(send)
        backs.append(permute(send, lambda z, x, y, c: (z, x, 1 - y, c)))
        return [total[:, :half] for total in totals], len(backs) - 1

    def reduce(totals, j):
        back = after(backs[j], leaving[-1]) if leaving else backs[j]
        near, far = swap_if(flip, *[total + b for total, b in zip(totals, back)])
        back = permute(far.astype(jnp.bfloat16), lambda z, x, y, c: (z ^ 1, x, y, c))
        near = near + after(back, *sends[j + 3 : j + 4])
        send = near[part:].astype(jnp.bfloat16)
        leaving.append(send)
        back = permute(send, lambda z, x, y, c: (z ^ 2, x, y, c))
        result.append((near[:part] + back).astype(jnp.bfloat16))

    update(0, own[0])
    to_plane(0)
    gather(0)
    update(1)
    gather(1)
    update(2, pairs[0])
    update(3, crossed[0])
    to_cores(0, used[1])
    to_plane(1, *moved[0])
    gather(2)
    jobs = [multiply(0, 0), multiply(0, 1)]
    gather(3, backs[0], sends[1])
    jobs.append(multiply(0, 2))
    jobs.append(multiply(0, 3))
    to_cores(1, sends[3])
    jobs += [multiply(1, q) for q in range(COL_CHUNKS)]
    for job in jobs:
        reduce(*job)
    result = [jnp.concatenate(result[i : i + COL_CHUNKS], axis=1) for i in range(0, len(result), COL_CHUNKS)]
    decoded = jnp.concatenate(result, axis=0)
    return (*updated, decoded)


def solution(mesh):
    placed = (
        P(("fsdp", "tp"), None),
        P(("fsdp", "tp"), None),
        P(("fsdp", "tp"), None),
        P(("fsdp", "tp"), None),
        P("fsdp", "tp"),
    )
    return jax.shard_map(
        local,
        mesh=mesh,
        in_specs=placed,
        out_specs=(
            P(("fsdp", "tp"), None),
            P(("fsdp", "tp"), None),
            P(("fsdp", "tp"), None),
            P("fsdp", "tp"),
        ),
        check_vma=False,
    )
```

```python
import jax
import jax.numpy as jnp
from jax import lax
from jax.experimental import pallas as pl
from jax.experimental.pallas import tpu as pltpu
from jax.sharding import PartitionSpec as P

AXES = ("fsdp", "tp")
ROW_CHUNKS = 2
CHUNKS = ((0, 1), (1, 1), (2, 2))


def adam(where, chunks, args, previous):
    rows, cols = args[0].shape
    widths = [cols // 16 * count for first, count in chunks]
    width = sum(widths)
    step = max(s for s in range(16, 449, 16) if rows % s == 0)
    tiles = rows // step
    spread = cols // 4 // width
    start = chunks[0][0] * (cols // 16) // width

    def kernel(where_ref, master_ref, one_ref, two_ref, grad_ref, *refs):
        outs = refs[-3 - len(chunks) :]
        grad = grad_ref[...].astype(jnp.float32)
        new_one = 0.9 * one_ref[...] + 0.1 * grad
        new_two = 0.95 * two_ref[...] + 0.05 * grad * grad
        new_master = master_ref[...] - 0.001 * new_one / (jnp.sqrt(new_two) + 1e-08)
        outs[0][...] = new_master
        outs[1][...] = new_one
        outs[2][...] = new_two
        at = 0
        for ref, size in zip(outs[3:], widths):
            ref[...] = new_master[:, at : at + size].astype(jnp.bfloat16)
            at += size

    def at(i, w):
        return i % tiles, i // tiles * spread + start

    def piece_at(i, w):
        j = i // tiles
        return i % tiles, 2 * ((j % 2) ^ w[1]) + ((j // 2) ^ w[0])

    block = pl.BlockSpec((step, width), at)
    full = jax.ShapeDtypeStruct((rows, cols), jnp.float32)
    size = 4 * rows * width
    out = pl.pallas_call(
        kernel,
        grid_spec=pltpu.PrefetchScalarGridSpec(
            num_scalar_prefetch=1,
            grid=(4 * tiles,),
            in_specs=[block] * 4 + [pl.BlockSpec(memory_space=pl.ANY)] * len(previous),
            out_specs=[block] * 3 + [pl.BlockSpec((step, size), piece_at) for size in widths],
        ),
        out_shape=[full] * 3 + [jax.ShapeDtypeStruct((rows, 4 * size), jnp.bfloat16) for size in widths],
        input_output_aliases={5 + i: i for i in range(len(previous))},
        compiler_params=pltpu.CompilerParams(vmem_limit_bytes=60 * 1024 * 1024),
        cost_estimate=pl.CostEstimate(flops=12 * size, bytes_accessed=28 * size, transcendentals=size),
        name="adam",
    )(where, *args, *previous)
    return out[:3], out[3:]


def pack(where, act, xs):
    rows, cols = act.shape
    run = cols // xs // 2
    part = rows // ROW_CHUNKS

    def kernel(where_ref, act_ref, *out_refs):
        for y in range(2):
            for x in range(xs):

                @pl.when((where_ref[0] == y) & (where_ref[2] == x))
                def _():
                    for m in range(ROW_CHUNKS):
                        for s in range(2):
                            for d in range(xs):
                                at = (2 * (x ^ d) + (y ^ s)) * run
                                out_refs[2 * m + s][:, d * run : (d + 1) * run] = act_ref[
                                    m * part : (m + 1) * part, at : at + run
                                ]

    out = pl.pallas_call(
        kernel,
        in_specs=[pl.BlockSpec(memory_space=pltpu.SMEM), pl.BlockSpec(memory_space=pltpu.VMEM)],
        out_specs=[pl.BlockSpec(memory_space=pltpu.VMEM)] * (2 * ROW_CHUNKS),
        out_shape=[jax.ShapeDtypeStruct((part, cols // 2), act.dtype)] * (2 * ROW_CHUNKS),
        compiler_params=pltpu.CompilerParams(vmem_limit_bytes=32 * 1024 * 1024),
        cost_estimate=pl.CostEstimate(flops=0, bytes_accessed=4 * rows * cols, transcendentals=0),
        name="pack",
    )(where, act)
    return out[0::2], out[1::2]


def swap_if(flag, low, high):
    return jnp.where(flag, high, low), jnp.where(flag, low, high)


def after(value, *done):
    return lax.optimization_barrier((value, *done))[0] if done else value


def local(master, moment_one, moment_two, gradient, hidden_act):
    fsdp, tp = lax.axis_size("fsdp"), lax.axis_size("tp")
    xs = fsdp // tp
    f, t = lax.axis_index("fsdp"), lax.axis_index("tp")
    z, x, y, c = f // xs, f % xs, t // 2, t % 2
    where = jnp.stack([y, c, x]).astype(jnp.int32)

    def permute(value, to):
        pairs = []
        for zi in range(tp):
            for xi in range(xs):
                for yi in range(2):
                    for ci in range(2):
                        zo, xo, yo, co = to(zi, xi, yi, ci)
                        pairs.append(((zi * xs + xi) * tp + 2 * yi + ci, (zo * xs + xo) * tp + 2 * yo + co))
        return lax.ppermute(value, AXES, pairs)

    rows = hidden_act.shape[0]
    part = rows // ROW_CHUNKS
    own, other = pack(where, hidden_act, xs)

    args = (master, moment_one, moment_two, gradient)
    updated, pieces = [], []

    def update(chunks, *done):
        new, weights = adam(after(where, *done), chunks, args, updated)
        updated[:] = new
        pieces.extend(weights)

    flip = (c ^ (z % 2)) != 0
    crossed, used, tables = [], [], []
    theirs, pairs, moved, acts = [], [], [], []
    sends, backs, leaving, result = [], [], [], []

    def cross(m):
        theirs.append(permute(other[m], lambda z, x, y, c: (z, x, 1 - y, c)))

    def to_plane(m, *done):
        pair = after(swap_if(((z // 2) ^ y) != 0, own[m], theirs[m]), *done)
        pairs.append(pair)
        moved.append(
            [permute(data, lambda z, x, y, c: (2 * ((z // 2) ^ a) + c, x, y, z % 2)) for a, data in enumerate(pair)]
        )

    def to_cores(m, *done):
        got = after(moved[m], *done)
        acts.append(got + [permute(data, lambda z, x, y, c: (z, x, y, 1 - c)) for data in got])

    def gather(q, *done):
        piece = after(pieces[q], *done)
        crossed.append([piece] + [permute(piece, lambda z, x, y, c: (z, x ^ d, y, c)) for d in range(1, xs)])

    def to_table(q, *done):
        parts = after(crossed[q], *done)
        half = parts[0].shape[1] // 2
        width = half // CHUNKS[q][1]
        near = jnp.stack([p[:, :half] for p in parts])
        far = []
        for at in range(half, 2 * half, width):
            there = jnp.stack([p[:, at : at + width] for p in parts])
            far.append(permute(there, lambda z, x, y, c: (z, x, y, 1 - c)))
        far = jnp.concatenate(far, axis=2)
        tables.append(jnp.stack(swap_if(c != 0, near, far), axis=1).reshape(-1, half))

    def multiply(m, q, *done):
        table = after(tables[q], *done)
        half = table.shape[1] // 2
        totals = [jnp.dot(a, table, preferred_element_type=jnp.float32) for a in acts[m]]
        width = half // CHUNKS[q][1]
        jobs = []
        for at in range(0, half, width):
            send = jnp.stack([total[:, half + at : half + at + width].astype(jnp.bfloat16) for total in totals])
            send = after(send, *sends[-1:], *backs[-2:-1])
            sends.append(send)
            backs.append(permute(send, lambda z, x, y, c: (z, x, 1 - y, c)))
            jobs.append(([total[:, at : at + width] for total in totals], len(backs) - 1))
        return jobs

    def reduce(totals, j):
        back = after(backs[j], leaving[-1]) if leaving else backs[j]
        totals = [total + b for total, b in zip(totals, back)]
        near, far = zip(*[swap_if(flip, own, sibling) for own, sibling in zip(totals[:2], totals[2:])])
        back = permute(jnp.stack(far).astype(jnp.bfloat16), lambda z, x, y, c: (z ^ 1, x, y, c))
        back = after(back, *sends[j + 3 : j + 4])
        send = (near[1] + back[1]).astype(jnp.bfloat16)
        leaving.append(send)
        back = near[0] + back[0] + permute(send, lambda z, x, y, c: (z ^ 2, x, y, c))
        result.append(back.astype(jnp.bfloat16))

    update(CHUNKS[:2], own[0])
    cross(0)
    cross(1)
    gather(0)
    gather(1)
    update(CHUNKS[2:])
    to_plane(0, pieces[2])
    gather(2, crossed[0][-1])
    to_table(0)
    to_table(1)
    to_cores(0)
    to_plane(1, *moved[0])
    jobs = multiply(0, 0) + multiply(0, 1)
    to_table(2, backs[0])
    jobs += multiply(0, 2)
    to_cores(1, backs[2])
    for q in range(len(CHUNKS)):
        jobs += multiply(1, q)
    for job in jobs:
        reduce(*job)
    count = len(result) // ROW_CHUNKS
    result = [jnp.concatenate(result[i : i + count], axis=1) for i in range(0, len(result), count)]
    decoded = jnp.concatenate(result, axis=0)
    return (*updated, decoded)


def solution(mesh):
    placed = (
        P(("fsdp", "tp"), None),
        P(("fsdp", "tp"), None),
        P(("fsdp", "tp"), None),
        P(("fsdp", "tp"), None),
        P("fsdp", "tp"),
    )
    return jax.shard_map(
        local,
        mesh=mesh,
        in_specs=placed,
        out_specs=(
            P(("fsdp", "tp"), None),
            P(("fsdp", "tp"), None),
            P(("fsdp", "tp"), None),
            P("fsdp", "tp"),
        ),
        check_vma=False,
    )
```

```python
import jax
import jax.numpy as jnp
from jax import lax
from jax.experimental import pallas as pl
from jax.experimental.pallas import tpu as pltpu
from jax.sharding import PartitionSpec as P

AXES = ("fsdp", "tp")
ROW_CHUNKS = 2
CHUNKS = ((0, 1), (1, 1), (2, 2))


def adam(where, chunks, args, previous):
    rows, cols = args[0].shape
    unit = cols // 16
    counts = [count for first, count in chunks]
    width = unit * sum(counts)
    step = max(s for s in range(16, 449, 16) if rows % s == 0)
    tiles = rows // step
    spread = cols // 4 // width
    start = chunks[0][0] * unit // width

    def kernel(where_ref, master_ref, one_ref, two_ref, grad_ref, *refs):
        outs = refs[-3 - len(chunks) :]
        grad = grad_ref[...].astype(jnp.float32)
        new_one = 0.9 * one_ref[...] + 0.1 * grad
        new_two = 0.95 * two_ref[...] + 0.05 * grad * grad
        new_master = master_ref[...] - 0.001 * new_one / (jnp.sqrt(new_two) + 1e-08)
        outs[0][...] = new_master
        outs[1][...] = new_one
        outs[2][...] = new_two
        at = 0
        for ref, count in zip(outs[3:], counts):
            for k in range(count):
                ref[k] = new_master[:, at : at + unit].astype(jnp.bfloat16)
                at += unit

    def at(i, w):
        return i % tiles, i // tiles * spread + start

    def piece_at(i, w):
        j = i // tiles
        return 0, i % tiles, 2 * ((j % 2) ^ w[1]) + ((j // 2) ^ w[0])

    block = pl.BlockSpec((step, width), at)
    full = jax.ShapeDtypeStruct((rows, cols), jnp.float32)
    size = 4 * rows * width
    out = pl.pallas_call(
        kernel,
        grid_spec=pltpu.PrefetchScalarGridSpec(
            num_scalar_prefetch=1,
            grid=(4 * tiles,),
            in_specs=[block] * 4 + [pl.BlockSpec(memory_space=pl.ANY)] * len(previous),
            out_specs=[block] * 3 + [pl.BlockSpec((count, step, unit), piece_at) for count in counts],
        ),
        out_shape=[full] * 3 + [jax.ShapeDtypeStruct((count, rows, 4 * unit), jnp.bfloat16) for count in counts],
        input_output_aliases={5 + i: i for i in range(len(previous))},
        compiler_params=pltpu.CompilerParams(vmem_limit_bytes=60 * 1024 * 1024),
        cost_estimate=pl.CostEstimate(flops=12 * size, bytes_accessed=28 * size, transcendentals=size),
        name="adam",
    )(where, *args, *previous)
    return out[:3], out[3:]


def pack(where, act, xs):
    rows, cols = act.shape
    run = cols // xs // 2
    part = rows // ROW_CHUNKS

    def kernel(where_ref, act_ref, *out_refs):
        for y in range(2):
            for x in range(xs):

                @pl.when((where_ref[0] == y) & (where_ref[2] == x))
                def _():
                    for m in range(ROW_CHUNKS):
                        for s in range(2):
                            for d in range(xs):
                                at = (2 * (x ^ d) + (y ^ s)) * run
                                out_refs[2 * m + s][:, d * run : (d + 1) * run] = act_ref[
                                    m * part : (m + 1) * part, at : at + run
                                ]

    out = pl.pallas_call(
        kernel,
        in_specs=[pl.BlockSpec(memory_space=pltpu.SMEM), pl.BlockSpec(memory_space=pltpu.VMEM)],
        out_specs=[pl.BlockSpec(memory_space=pltpu.VMEM)] * (2 * ROW_CHUNKS),
        out_shape=[jax.ShapeDtypeStruct((part, cols // 2), act.dtype)] * (2 * ROW_CHUNKS),
        compiler_params=pltpu.CompilerParams(vmem_limit_bytes=32 * 1024 * 1024),
        cost_estimate=pl.CostEstimate(flops=0, bytes_accessed=4 * rows * cols, transcendentals=0),
        name="pack",
    )(where, act)
    return out[0::2], out[1::2]


def swap_if(flag, low, high):
    return jnp.where(flag, high, low), jnp.where(flag, low, high)


def after(value, *done):
    return lax.optimization_barrier((value, *done))[0] if done else value


def local(master, moment_one, moment_two, gradient, hidden_act):
    fsdp, tp = lax.axis_size("fsdp"), lax.axis_size("tp")
    xs = fsdp // tp
    f, t = lax.axis_index("fsdp"), lax.axis_index("tp")
    z, x, y, c = f // xs, f % xs, t // 2, t % 2
    where = jnp.stack([y, c, x]).astype(jnp.int32)

    def permute(value, to):
        pairs = []
        for zi in range(tp):
            for xi in range(xs):
                for yi in range(2):
                    for ci in range(2):
                        zo, xo, yo, co = to(zi, xi, yi, ci)
                        pairs.append(((zi * xs + xi) * tp + 2 * yi + ci, (zo * xs + xo) * tp + 2 * yo + co))
        return lax.ppermute(value, AXES, pairs)

    rows = hidden_act.shape[0]
    part = rows // ROW_CHUNKS
    own, other = pack(where, hidden_act, xs)

    args = (master, moment_one, moment_two, gradient)
    updated, pieces = [], []

    def update(chunks, *done):
        new, weights = adam(after(where, *done), chunks, args, updated)
        updated[:] = new
        pieces.extend(weights)

    flip = (c ^ (z % 2)) != 0
    crossed, tables = [], []
    theirs, pairs, moved, acts = [], [], [], []
    jobs, sends, backs = [], [], []
    nears, fars, halfway, leaving, result = [], [], [], [], []

    def cross(m, *done):
        theirs.append(permute(after(other[m], *done), lambda z, x, y, c: (z, x, 1 - y, c)))

    def to_plane(m, *done):
        pair = after(swap_if(((z // 2) ^ y) != 0, own[m], theirs[m]), *done)
        pairs.append(pair)
        moved.append(
            [permute(data, lambda z, x, y, c: (2 * ((z // 2) ^ a) + c, x, y, z % 2)) for a, data in enumerate(pair)]
        )

    def to_cores(m, *done):
        got = after(moved[m], *done)
        acts.append(got + [permute(data, lambda z, x, y, c: (z, x, y, 1 - c)) for data in got])

    def gather(q, *done):
        piece = after(pieces[q], *done)
        crossed.append([piece] + [permute(piece, lambda z, x, y, c: (z, x ^ d, y, c)) for d in range(1, xs)])

    def to_tables(q, *done):
        parts = after(crossed[q], *done)
        half = parts[0].shape[2] // 2
        for k in range(parts[0].shape[0]):
            near = jnp.stack([p[k, :, :half] for p in parts])
            far = jnp.stack([p[k, :, half:] for p in parts])
            far = permute(far, lambda z, x, y, c: (z, x, y, 1 - c))
            tables.append(jnp.stack(swap_if(c != 0, near, far), axis=1).reshape(-1, half))

    def multiply(m, q, pieces=1):
        half = tables[q].shape[1] // 2
        totals = [jnp.dot(a, tables[q], preferred_element_type=jnp.float32) for a in acts[m]]
        width = half // pieces
        for at in range(0, half, width):
            send = jnp.stack([total[:, half + at : half + at + width].astype(jnp.bfloat16) for total in totals])
            send = after(send, *sends[-1:], *backs[-2:-1])
            sends.append(send)
            backs.append(permute(send, lambda z, x, y, c: (z, x, 1 - y, c)))
            jobs.append([total[:, at : at + width] for total in totals])

    def step_one(j):
        back = after(backs[j], *leaving[j - 1 : j])
        totals = [total + b for total, b in zip(jobs[j], back)]
        count = len(totals) // 2
        near, far = zip(*[swap_if(flip, own, sibling) for own, sibling in zip(totals[:count], totals[count:])])
        near, far = [jnp.concatenate(v, axis=0) if count > 1 else v[0] for v in (near, far)]
        nears.append(near)
        fars.append(far.astype(jnp.bfloat16))
        halfway.append(permute(fars[j], lambda z, x, y, c: (z ^ 1, x, y, c)))

    def step_two(j):
        back = after(halfway[j], *sends[j + 3 : j + 4])
        total = nears[j] + back
        leaving.append(total[part:].astype(jnp.bfloat16))
        nears[j] = total[:part]
        halfway[j] = permute(leaving[j], lambda z, x, y, c: (z ^ 2, x, y, c))

    def step_three(j):
        result.append((nears[j] + halfway[j]).astype(jnp.bfloat16))

    update(CHUNKS[:2], own[0])
    cross(0)
    cross(1)
    gather(0)
    gather(1)
    update(CHUNKS[2:])
    to_plane(0, pieces[2])
    gather(2, crossed[0][-1])
    to_tables(0)
    to_tables(1)
    to_cores(0)
    to_plane(1, *moved[0])
    multiply(0, 0)
    multiply(0, 1)
    to_tables(2, backs[0])
    multiply(0, 2)
    multiply(0, 3)
    to_cores(1, backs[2])
    for q in range(4):
        multiply(1, q, 1 + q // 3)
    count = len(jobs)
    for j in range(count + 1):
        if j >= 1:
            step_two(j - 1)
        if j < count:
            step_one(j)
        if j >= 1:
            step_three(j - 1)
    result = [jnp.concatenate(result[:4], axis=1), jnp.concatenate(result[4:], axis=1)]
    decoded = jnp.concatenate(result, axis=0)
    return (*updated, decoded)


def solution(mesh):
    placed = (
        P(("fsdp", "tp"), None),
        P(("fsdp", "tp"), None),
        P(("fsdp", "tp"), None),
        P(("fsdp", "tp"), None),
        P("fsdp", "tp"),
    )
    return jax.shard_map(
        local,
        mesh=mesh,
        in_specs=placed,
        out_specs=(
            P(("fsdp", "tp"), None),
            P(("fsdp", "tp"), None),
            P(("fsdp", "tp"), None),
            P("fsdp", "tp"),
        ),
        check_vma=False,
    )
```

```python
import jax
import jax.numpy as jnp
from jax import lax
from jax.experimental import pallas as pl
from jax.experimental.pallas import tpu as pltpu
from jax.sharding import PartitionSpec as P

AXES = ("fsdp", "tp")
ROW_CHUNKS = 2
CHUNKS = ((0, 1), (1, 1), (2, 2))


def adam(where, chunks, args, previous):
    rows, cols = args[0].shape
    unit = cols // 16
    counts = [count for first, count in chunks]
    width = unit * sum(counts)
    step = max(s for s in range(16, 225, 16) if rows % s == 0)
    tiles = rows // step
    spread = cols // 4 // width
    start = chunks[0][0] * unit // width

    def kernel(where_ref, master_ref, one_ref, two_ref, grad_ref, *refs):
        outs = refs[-3 - len(chunks) :]
        grad = grad_ref[...].astype(jnp.float32)
        new_one = 0.9 * one_ref[...] + 0.1 * grad
        new_two = 0.95 * two_ref[...] + 0.05 * grad * grad
        new_master = master_ref[...] - 0.001 * new_one / (jnp.sqrt(new_two) + 1e-08)
        outs[0][...] = new_master
        outs[1][...] = new_one
        outs[2][...] = new_two
        at = 0
        for ref, count in zip(outs[3:], counts):
            for k in range(count):
                ref[k] = new_master[:, at : at + unit].astype(jnp.bfloat16)
                at += unit

    def at(i, w):
        return i % tiles, i // tiles * spread + start

    def piece_at(i, w):
        j = i // tiles
        return 0, i % tiles, 2 * ((j % 2) ^ w[1]) + ((j // 2) ^ w[0])

    block = pl.BlockSpec((step, width), at)
    full = jax.ShapeDtypeStruct((rows, cols), jnp.float32)
    size = 4 * rows * width
    out = pl.pallas_call(
        kernel,
        grid_spec=pltpu.PrefetchScalarGridSpec(
            num_scalar_prefetch=1,
            grid=(4 * tiles,),
            in_specs=[block] * 4 + [pl.BlockSpec(memory_space=pl.ANY)] * len(previous),
            out_specs=[block] * 3 + [pl.BlockSpec((count, step, unit), piece_at) for count in counts],
        ),
        out_shape=[full] * 3 + [jax.ShapeDtypeStruct((count, rows, 4 * unit), jnp.bfloat16) for count in counts],
        input_output_aliases={5 + i: i for i in range(len(previous))},
        compiler_params=pltpu.CompilerParams(vmem_limit_bytes=60 * 1024 * 1024),
        cost_estimate=pl.CostEstimate(flops=12 * size, bytes_accessed=28 * size, transcendentals=size),
        name="adam",
    )(where, *args, *previous)
    return out[:3], out[3:]


def pack(where, act, xs):
    rows, cols = act.shape
    run = cols // xs // 2
    part = rows // ROW_CHUNKS

    def kernel(where_ref, act_ref, *out_refs):
        for y in range(2):
            for x in range(xs):

                @pl.when((where_ref[0] == y) & (where_ref[2] == x))
                def _():
                    for m in range(ROW_CHUNKS):
                        for s in range(2):
                            for d in range(xs):
                                at = (2 * (x ^ d) + (y ^ s)) * run
                                out_refs[2 * m + s][:, d * run : (d + 1) * run] = act_ref[
                                    m * part : (m + 1) * part, at : at + run
                                ]

    out = pl.pallas_call(
        kernel,
        in_specs=[pl.BlockSpec(memory_space=pltpu.SMEM), pl.BlockSpec(memory_space=pltpu.VMEM)],
        out_specs=[pl.BlockSpec(memory_space=pltpu.VMEM)] * (2 * ROW_CHUNKS),
        out_shape=[jax.ShapeDtypeStruct((part, cols // 2), act.dtype)] * (2 * ROW_CHUNKS),
        compiler_params=pltpu.CompilerParams(vmem_limit_bytes=32 * 1024 * 1024),
        cost_estimate=pl.CostEstimate(flops=0, bytes_accessed=4 * rows * cols, transcendentals=0),
        name="pack",
    )(where, act)
    return out[0::2], out[1::2]


def swap_if(flag, low, high):
    return jnp.where(flag, high, low), jnp.where(flag, low, high)


def after(value, *done):
    return lax.optimization_barrier((value, *done))[0] if done else value


def local(master, moment_one, moment_two, gradient, hidden_act):
    fsdp, tp = lax.axis_size("fsdp"), lax.axis_size("tp")
    xs = fsdp // tp
    f, t = lax.axis_index("fsdp"), lax.axis_index("tp")
    z, x, y, c = f // xs, f % xs, t // 2, t % 2
    where = jnp.stack([y, c, x]).astype(jnp.int32)

    def permute(value, to):
        pairs = []
        for zi in range(tp):
            for xi in range(xs):
                for yi in range(2):
                    for ci in range(2):
                        zo, xo, yo, co = to(zi, xi, yi, ci)
                        pairs.append(((zi * xs + xi) * tp + 2 * yi + ci, (zo * xs + xo) * tp + 2 * yo + co))
        return lax.ppermute(value, AXES, pairs)

    rows = hidden_act.shape[0]
    part = rows // ROW_CHUNKS
    own, other = pack(where, hidden_act, xs)

    args = (master, moment_one, moment_two, gradient)
    updated, pieces = [], []

    def update(chunks, *done):
        new, weights = adam(after(where, *done), chunks, args, updated)
        updated[:] = new
        pieces.extend(weights)

    flip = (c ^ (z % 2)) != 0
    crossed, tables = [], []
    theirs, pairs, moved, acts = [], [], [], []
    jobs, sends, backs = [], [], []
    nears, fars, halfway, leaving, result = [], [], [], [], []

    def cross(m, *done):
        theirs.append(permute(after(other[m], *done), lambda z, x, y, c: (z, x, 1 - y, c)))

    def to_plane(m, *done):
        pair = after(swap_if(((z // 2) ^ y) != 0, own[m], theirs[m]), *done)
        pairs.append(pair)
        moved.append(
            [permute(data, lambda z, x, y, c: (2 * ((z // 2) ^ a) + c, x, y, z % 2)) for a, data in enumerate(pair)]
        )

    def to_cores(m, *done):
        got = after(moved[m], *done)
        acts.append(got + [permute(data, lambda z, x, y, c: (z, x, y, 1 - c)) for data in got])

    def gather(q, *done):
        piece = after(pieces[q], *done)
        crossed.append([piece] + [permute(piece, lambda z, x, y, c: (z, x ^ d, y, c)) for d in range(1, xs)])

    def to_tables(q, *done):
        parts = after(crossed[q], *done)
        half = parts[0].shape[2] // 2
        for k in range(parts[0].shape[0]):
            near = jnp.stack([p[k, :, :half] for p in parts])
            far = jnp.stack([p[k, :, half:] for p in parts])
            far = permute(far, lambda z, x, y, c: (z, x, y, 1 - c))
            tables.append(jnp.stack(swap_if(c != 0, near, far), axis=1).reshape(-1, half))

    early = 5

    def multiply(m, q, pieces=1):
        half = tables[q].shape[1] // 2
        totals = [jnp.dot(a, tables[q], preferred_element_type=jnp.float32) for a in acts[m]]
        width = half // pieces
        for at in range(0, half, width):
            send = jnp.stack([total[:, half + at : half + at + width].astype(jnp.bfloat16) for total in totals])
            send = after(send, *sends[-1:], *backs[-2:-1])
            sends.append(send)
            backs.append(permute(send, lambda z, x, y, c: (z, x, 1 - y, c)))
            jobs.append([total[:, at : at + width] for total in totals])

    def step_one(j):
        done = leaving[j - 1 : j] if j <= early else leaving[j - 2 : j - 1]
        back = after(backs[j], *done)
        totals = [total + b for total, b in zip(jobs[j], back)]
        count = len(totals) // 2
        near, far = zip(*[swap_if(flip, own, sibling) for own, sibling in zip(totals[:count], totals[count:])])
        near, far = [jnp.concatenate(v, axis=0) if count > 1 else v[0] for v in (near, far)]
        nears.append(near)
        fars.append(far.astype(jnp.bfloat16))
        halfway.append(permute(fars[j], lambda z, x, y, c: (z ^ 1, x, y, c)))

    def step_two(j):
        back = after(halfway[j], *sends[j + 3 : j + 4])
        total = nears[j] + back
        leaving.append(total[part:].astype(jnp.bfloat16))
        nears[j] = total[:part]
        halfway[j] = permute(leaving[j], lambda z, x, y, c: (z ^ 2, x, y, c))

    def step_three(j):
        result.append((nears[j] + halfway[j]).astype(jnp.bfloat16))

    update(CHUNKS[:2], own[0])
    cross(0)
    cross(1)
    gather(0)
    gather(1)
    update(CHUNKS[2:])
    to_plane(0, pieces[2])
    gather(2, crossed[0][-1])
    to_tables(0)
    to_tables(1)
    to_cores(0)
    to_plane(1, *moved[0])
    multiply(0, 0)
    multiply(0, 1)
    to_tables(2, backs[0], moved[1][0])
    multiply(0, 2)
    multiply(0, 3)
    to_cores(1, backs[2])
    for q in range(4):
        multiply(1, q, 1 + q // 3)
    count = len(jobs)
    for j in range(count + 2):
        if j <= early and 1 <= j <= count:
            step_two(j - 1)
        if j < count:
            step_one(j)
        if j > early and j <= count:
            step_two(j - 1)
        if j >= 2:
            step_three(j - 2)
    result = [jnp.concatenate(result[:4], axis=1), jnp.concatenate(result[4:], axis=1)]
    decoded = jnp.concatenate(result, axis=0)
    return (*updated, decoded)


def solution(mesh):
    placed = (
        P(("fsdp", "tp"), None),
        P(("fsdp", "tp"), None),
        P(("fsdp", "tp"), None),
        P(("fsdp", "tp"), None),
        P("fsdp", "tp"),
    )
    return jax.shard_map(
        local,
        mesh=mesh,
        in_specs=placed,
        out_specs=(
            P(("fsdp", "tp"), None),
            P(("fsdp", "tp"), None),
            P(("fsdp", "tp"), None),
            P("fsdp", "tp"),
        ),
        check_vma=False,
    )
```

```python
import jax
import jax.numpy as jnp
from jax import lax
from jax.experimental import pallas as pl
from jax.experimental.pallas import tpu as pltpu
from jax.sharding import PartitionSpec as P

AXES = ("fsdp", "tp")
ROW_CHUNKS = 2
CHUNKS = ((0, 1), (1, 1), (2, 2))


def adam(where, chunks, args, previous):
    rows, cols = args[0].shape
    unit = cols // 16
    counts = [count for first, count in chunks]
    width = unit * sum(counts)
    step = max(s for s in range(16, 449, 16) if rows % s == 0)
    tiles = rows // step
    spread = cols // 4 // width
    start = chunks[0][0] * unit // width

    def kernel(where_ref, master_ref, one_ref, two_ref, grad_ref, *refs):
        outs = refs[-3 - len(chunks) :]
        grad = grad_ref[...].astype(jnp.float32)
        new_one = 0.9 * one_ref[...] + 0.1 * grad
        new_two = 0.95 * two_ref[...] + 0.05 * grad * grad
        new_master = master_ref[...] - 0.001 * new_one / (jnp.sqrt(new_two) + 1e-08)
        outs[0][...] = new_master
        outs[1][...] = new_one
        outs[2][...] = new_two
        at = 0
        for ref, count in zip(outs[3:], counts):
            for k in range(count):
                ref[k] = new_master[:, at : at + unit].astype(jnp.bfloat16)
                at += unit

    def at(i, w):
        return i % tiles, i // tiles * spread + start

    def piece_at(i, w):
        j = i // tiles
        return 0, i % tiles, 2 * ((j % 2) ^ w[1]) + ((j // 2) ^ w[0])

    block = pl.BlockSpec((step, width), at)
    full = jax.ShapeDtypeStruct((rows, cols), jnp.float32)
    size = 4 * rows * width
    out = pl.pallas_call(
        kernel,
        grid_spec=pltpu.PrefetchScalarGridSpec(
            num_scalar_prefetch=1,
            grid=(4 * tiles,),
            in_specs=[block] * 4 + [pl.BlockSpec(memory_space=pl.ANY)] * len(previous),
            out_specs=[block] * 3 + [pl.BlockSpec((count, step, unit), piece_at) for count in counts],
        ),
        out_shape=[full] * 3 + [jax.ShapeDtypeStruct((count, rows, 4 * unit), jnp.bfloat16) for count in counts],
        input_output_aliases={5 + i: i for i in range(len(previous))},
        compiler_params=pltpu.CompilerParams(vmem_limit_bytes=60 * 1024 * 1024),
        cost_estimate=pl.CostEstimate(flops=12 * size, bytes_accessed=28 * size, transcendentals=size),
        name="adam",
    )(where, *args, *previous)
    return out[:3], out[3:]


def pack(where, act, xs):
    rows, cols = act.shape
    run = cols // xs // 2
    part = rows // ROW_CHUNKS

    def kernel(where_ref, act_ref, *out_refs):
        for y in range(2):
            for x in range(xs):

                @pl.when((where_ref[0] == y) & (where_ref[2] == x))
                def _():
                    for m in range(ROW_CHUNKS):
                        for s in range(2):
                            for d in range(xs):
                                at = (2 * (x ^ d) + (y ^ s)) * run
                                out_refs[2 * m + s][:, d * run : (d + 1) * run] = act_ref[
                                    m * part : (m + 1) * part, at : at + run
                                ]

    out = pl.pallas_call(
        kernel,
        in_specs=[pl.BlockSpec(memory_space=pltpu.SMEM), pl.BlockSpec(memory_space=pltpu.VMEM)],
        out_specs=[pl.BlockSpec(memory_space=pltpu.VMEM)] * (2 * ROW_CHUNKS),
        out_shape=[jax.ShapeDtypeStruct((part, cols // 2), act.dtype)] * (2 * ROW_CHUNKS),
        compiler_params=pltpu.CompilerParams(vmem_limit_bytes=32 * 1024 * 1024),
        cost_estimate=pl.CostEstimate(flops=0, bytes_accessed=4 * rows * cols, transcendentals=0),
        name="pack",
    )(where, act)
    return out[0::2], out[1::2]


def swap_if(flag, low, high):
    return jnp.where(flag, high, low), jnp.where(flag, low, high)


def after(value, *done):
    return lax.optimization_barrier((value, *done))[0] if done else value


def local(master, moment_one, moment_two, gradient, hidden_act):
    fsdp, tp = lax.axis_size("fsdp"), lax.axis_size("tp")
    xs = fsdp // tp
    f, t = lax.axis_index("fsdp"), lax.axis_index("tp")
    z, x, y, c = f // xs, f % xs, t // 2, t % 2
    where = jnp.stack([y, c, x]).astype(jnp.int32)

    def permute(value, to):
        pairs = []
        for zi in range(tp):
            for xi in range(xs):
                for yi in range(2):
                    for ci in range(2):
                        zo, xo, yo, co = to(zi, xi, yi, ci)
                        pairs.append(((zi * xs + xi) * tp + 2 * yi + ci, (zo * xs + xo) * tp + 2 * yo + co))
        return lax.ppermute(value, AXES, pairs)

    rows = hidden_act.shape[0]
    part = rows // ROW_CHUNKS
    own, other = pack(where, hidden_act, xs)

    args = (master, moment_one, moment_two, gradient)
    updated, pieces = [], []

    def update(chunks, *done):
        new, weights = adam(after(where, *done), chunks, args, updated)
        updated[:] = new
        pieces.extend(weights)

    flip = (c ^ (z % 2)) != 0
    crossed, tables = [], []
    theirs, pairs, moved, acts = [], [], [], {}
    jobs, sends, backs = [], [], []
    nears, fars, halfway, summed, done_sums = [], [], [], [], []
    kept, result = [{}, {}], [{}, {}]

    def cross(m, *done):
        theirs.append(permute(after(other[m], *done), lambda z, x, y, c: (z, x, 1 - y, c)))

    def to_plane(m, *done):
        pair = after(swap_if(((z // 2) ^ y) != 0, own[m], theirs[m]), *done)
        pairs.append(pair)
        moved.append(
            [permute(data, lambda z, x, y, c: (2 * ((z // 2) ^ a) + c, x, y, z % 2)) for a, data in enumerate(pair)]
        )

    def to_cores(m, a, *done):
        got = after(moved[m][a], *done)
        acts[m, a] = (got, permute(got, lambda z, x, y, c: (z, x, y, 1 - c)))

    def gather(q, *done):
        piece = after(pieces[q], *done)
        crossed.append([piece] + [permute(piece, lambda z, x, y, c: (z, x ^ d, y, c)) for d in range(1, xs)])

    def to_tables(q, *done):
        parts = after(crossed[q], *done)
        half = parts[0].shape[2] // 2
        for k in range(parts[0].shape[0]):
            near = jnp.stack([p[k, :, :half] for p in parts])
            far = jnp.stack([p[k, :, half:] for p in parts])
            far = permute(far, lambda z, x, y, c: (z, x, y, 1 - c))
            tables.append(jnp.stack(swap_if(c != 0, near, far), axis=1).reshape(-1, half))

    early = 5

    def multiply(m, a, *columns):
        half = tables[0].shape[1] // 2
        totals = [
            [jnp.dot(act, tables[q], preferred_element_type=jnp.float32) for q in columns] for act in acts[m, a]
        ]
        send = jnp.stack(
            [jnp.concatenate([v[:, half:].astype(jnp.bfloat16) for v in total], axis=1) for total in totals]
        )
        send = after(send, *sends[-1:], *backs[-3:-2])
        sends.append(send)
        backs.append(permute(send, lambda z, x, y, c: (z, x, 1 - y, c)))
        jobs.append((m, a, columns, [jnp.concatenate([v[:, :half] for v in total], axis=1) for total in totals]))

    def step_one(j):
        done = summed[j - 1 : j] if j <= early else summed[j - 2 : j - 1]
        back = after(backs[j], *done)
        near, far = swap_if(flip, *[total + b for total, b in zip(jobs[j][3], back)])
        nears.append(near)
        fars.append(far.astype(jnp.bfloat16))
        halfway.append(permute(fars[j], lambda z, x, y, c: (z ^ 1, x, y, c)))

    def step_two(j):
        m, a, columns, _ = jobs[j]
        total = nears[j] + after(halfway[j], *sends[j + 3 : j + 4])
        if a == 1:
            total = total.astype(jnp.bfloat16)
            halfway[j] = permute(total, lambda z, x, y, c: (z ^ 2, x, y, c))
        summed.append(total)

    def step_three(j):
        m, a, columns, _ = jobs[j]
        width = summed[j].shape[1] // len(columns)
        for i, q in enumerate(columns):
            kept[m][q, a] = (halfway[j] if a else summed[j])[:, i * width : (i + 1) * width]
            if (q, 1 - a) in kept[m]:
                result[m][q] = (kept[m][q, 0] + kept[m][q, 1]).astype(jnp.bfloat16)

    update(CHUNKS[:2], own[0])
    cross(0)
    cross(1)
    gather(0)
    gather(1)
    update(CHUNKS[2:])
    to_plane(0, pieces[2])
    gather(2, crossed[1][-1])
    to_tables(0)
    to_tables(1)
    to_cores(0, 0, crossed[1][-1])
    to_cores(0, 1)
    to_plane(1, *moved[0])
    multiply(0, 0, 0, 1)
    multiply(0, 1, 0, 1)
    to_tables(2, backs[0], moved[1][0])
    multiply(0, 1, 2, 3)
    multiply(0, 0, 2, 3)
    to_cores(1, 0, backs[-2])
    to_cores(1, 1, sends[-1])
    multiply(1, 1, 0, 1)
    multiply(1, 1, 2, 3)
    multiply(1, 0, 0, 1)
    multiply(1, 0, 2, 3)
    count = len(jobs)
    for j in range(count + 2):
        if j <= early and 1 <= j <= count:
            step_two(j - 1)
        if j < count:
            step_one(j)
        if j > early and j <= count:
            step_two(j - 1)
        if j >= 2:
            step_three(j - 2)
    result = [jnp.concatenate([r[q] for q in sorted(r)], axis=1) for r in result]
    decoded = jnp.concatenate(result, axis=0)
    return (*updated, decoded)


def solution(mesh):
    placed = (
        P(("fsdp", "tp"), None),
        P(("fsdp", "tp"), None),
        P(("fsdp", "tp"), None),
        P(("fsdp", "tp"), None),
        P("fsdp", "tp"),
    )
    return jax.shard_map(
        local,
        mesh=mesh,
        in_specs=placed,
        out_specs=(
            P(("fsdp", "tp"), None),
            P(("fsdp", "tp"), None),
            P(("fsdp", "tp"), None),
            P("fsdp", "tp"),
        ),
        check_vma=False,
    )
```

```python
import jax
import jax.numpy as jnp
from jax import lax
from jax.experimental import pallas as pl
from jax.experimental.pallas import tpu as pltpu
from jax.sharding import PartitionSpec as P

AXES = ("fsdp", "tp")
ROW_CHUNKS = 2
CHUNKS = ((0, 1), (1, 1), (2, 2))


def adam(where, chunks, args, previous):
    rows, cols = args[0].shape
    unit = cols // 16
    counts = [count for first, count in chunks]
    width = unit * sum(counts)
    step = max(s for s in range(16, 449, 16) if rows % s == 0)
    tiles = rows // step
    spread = cols // 4 // width
    start = chunks[0][0] * unit // width

    def kernel(where_ref, master_ref, one_ref, two_ref, grad_ref, *refs):
        outs = refs[-3 - len(chunks) :]
        grad = grad_ref[...].astype(jnp.float32)
        new_one = 0.9 * one_ref[...] + 0.1 * grad
        new_two = 0.95 * two_ref[...] + 0.05 * grad * grad
        new_master = master_ref[...] - 0.001 * new_one / (jnp.sqrt(new_two) + 1e-08)
        outs[0][...] = new_master
        outs[1][...] = new_one
        outs[2][...] = new_two
        at = 0
        for ref, count in zip(outs[3:], counts):
            for k in range(count):
                ref[k] = new_master[:, at : at + unit].astype(jnp.bfloat16)
                at += unit

    def at(i, w):
        return i % tiles, i // tiles * spread + start

    def piece_at(i, w):
        j = i // tiles
        return 0, i % tiles, 2 * ((j % 2) ^ w[1]) + ((j // 2) ^ w[0])

    block = pl.BlockSpec((step, width), at)
    full = jax.ShapeDtypeStruct((rows, cols), jnp.float32)
    size = 4 * rows * width
    out = pl.pallas_call(
        kernel,
        grid_spec=pltpu.PrefetchScalarGridSpec(
            num_scalar_prefetch=1,
            grid=(4 * tiles,),
            in_specs=[block] * 4 + [pl.BlockSpec(memory_space=pl.ANY)] * len(previous),
            out_specs=[block] * 3 + [pl.BlockSpec((count, step, unit), piece_at) for count in counts],
        ),
        out_shape=[full] * 3 + [jax.ShapeDtypeStruct((count, rows, 4 * unit), jnp.bfloat16) for count in counts],
        input_output_aliases={5 + i: i for i in range(len(previous))},
        compiler_params=pltpu.CompilerParams(vmem_limit_bytes=60 * 1024 * 1024),
        cost_estimate=pl.CostEstimate(flops=12 * size, bytes_accessed=28 * size, transcendentals=size),
        name="adam",
    )(where, *args, *previous)
    return out[:3], out[3:]


def pack(where, act, xs):
    rows, cols = act.shape
    run = cols // xs // 2
    part = rows // ROW_CHUNKS

    def kernel(where_ref, act_ref, *out_refs):
        for y in range(2):
            for x in range(xs):

                @pl.when((where_ref[0] == y) & (where_ref[2] == x))
                def _():
                    for m in range(ROW_CHUNKS):
                        for s in range(2):
                            for d in range(xs):
                                at = (2 * (x ^ d) + (y ^ s)) * run
                                out_refs[2 * m + s][:, d * run : (d + 1) * run] = act_ref[
                                    m * part : (m + 1) * part, at : at + run
                                ]

    out = pl.pallas_call(
        kernel,
        in_specs=[pl.BlockSpec(memory_space=pltpu.SMEM), pl.BlockSpec(memory_space=pltpu.VMEM)],
        out_specs=[pl.BlockSpec(memory_space=pltpu.VMEM)] * (2 * ROW_CHUNKS),
        out_shape=[jax.ShapeDtypeStruct((part, cols // 2), act.dtype)] * (2 * ROW_CHUNKS),
        compiler_params=pltpu.CompilerParams(vmem_limit_bytes=32 * 1024 * 1024),
        cost_estimate=pl.CostEstimate(flops=0, bytes_accessed=4 * rows * cols, transcendentals=0),
        name="pack",
    )(where, act)
    return out[0::2], out[1::2]


def swap_if(flag, low, high):
    return jnp.where(flag, high, low), jnp.where(flag, low, high)


def after(value, *done):
    return lax.optimization_barrier((value, *done))[0] if done else value


def local(master, moment_one, moment_two, gradient, hidden_act):
    fsdp, tp = lax.axis_size("fsdp"), lax.axis_size("tp")
    xs = fsdp // tp
    f, t = lax.axis_index("fsdp"), lax.axis_index("tp")
    z, x, y, c = f // xs, f % xs, t // 2, t % 2
    where = jnp.stack([y, c, x]).astype(jnp.int32)

    def permute(value, to):
        pairs = []
        for zi in range(tp):
            for xi in range(xs):
                for yi in range(2):
                    for ci in range(2):
                        zo, xo, yo, co = to(zi, xi, yi, ci)
                        pairs.append(((zi * xs + xi) * tp + 2 * yi + ci, (zo * xs + xo) * tp + 2 * yo + co))
        return lax.ppermute(value, AXES, pairs)

    rows = hidden_act.shape[0]
    part = rows // ROW_CHUNKS
    own, other = pack(where, hidden_act, xs)

    args = (master, moment_one, moment_two, gradient)
    updated, pieces = [], []

    def update(chunks, *done):
        new, weights = adam(after(where, *done), chunks, args, updated)
        updated[:] = new
        pieces.extend(weights)

    flip = (c ^ (z % 2)) != 0
    crossed, tables = [], []
    theirs, pairs, moved, acts = [], [], [], []
    jobs, sends, backs = [], [], []
    nears, fars, halfway, leaving, result = [], [], [], [], []

    def cross(m, *done):
        theirs.append(permute(after(other[m], *done), lambda z, x, y, c: (z, x, 1 - y, c)))

    def to_plane(m, *done):
        pair = after(swap_if(((z // 2) ^ y) != 0, own[m], theirs[m]), *done)
        pairs.append(pair)
        moved.append(
            [permute(data, lambda z, x, y, c: (2 * ((z // 2) ^ a) + c, x, y, z % 2)) for a, data in enumerate(pair)]
        )

    def to_cores(m, *done):
        got = after(moved[m], *done)
        acts.append(got + [permute(data, lambda z, x, y, c: (z, x, y, 1 - c)) for data in got])

    def gather(q, *done):
        piece = after(pieces[q], *done)
        crossed.append([piece] + [permute(piece, lambda z, x, y, c: (z, x ^ d, y, c)) for d in range(1, xs)])

    def to_tables(q, *done):
        parts = after(crossed[q], *done)
        half = parts[0].shape[2] // 2
        for k in range(parts[0].shape[0]):
            near = jnp.stack([p[k, :, :half] for p in parts])
            far = jnp.stack([p[k, :, half:] for p in parts])
            far = permute(far, lambda z, x, y, c: (z, x, y, 1 - c))
            tables.append(jnp.stack(swap_if(c != 0, near, far), axis=1).reshape(-1, half))

    early = 5

    def multiply(m, q, pieces=1):
        half = tables[q].shape[1] // 2
        totals = [jnp.dot(a, tables[q], preferred_element_type=jnp.float32) for a in acts[m]]
        width = half // pieces
        for at in range(0, half, width):
            send = jnp.stack([total[:, half + at : half + at + width].astype(jnp.bfloat16) for total in totals])
            send = after(send, *sends[-1:], *backs[-2:-1])
            sends.append(send)
            backs.append(permute(send, lambda z, x, y, c: (z, x, 1 - y, c)))
            jobs.append([total[:, at : at + width] for total in totals])

    def step_one(j):
        done = leaving[j - 1 : j] if j <= early else leaving[j - 2 : j - 1]
        back = after(backs[j], *done)
        totals = [total + b for total, b in zip(jobs[j], back)]
        count = len(totals) // 2
        near, far = zip(*[swap_if(flip, own, sibling) for own, sibling in zip(totals[:count], totals[count:])])
        near, far = [jnp.concatenate(v, axis=0) if count > 1 else v[0] for v in (near, far)]
        nears.append(near)
        fars.append(far.astype(jnp.bfloat16))
        halfway.append(permute(fars[j], lambda z, x, y, c: (z ^ 1, x, y, c)))

    def step_two(j):
        back = after(halfway[j], *sends[j + 3 : j + 4])
        total = nears[j] + back
        leaving.append(total[part:].astype(jnp.bfloat16))
        nears[j] = total[:part]
        halfway[j] = permute(leaving[j], lambda z, x, y, c: (z ^ 2, x, y, c))

    def step_three(j):
        result.append((nears[j] + halfway[j]).astype(jnp.bfloat16))

    update(CHUNKS[:2], own[0])
    cross(0)
    cross(1)
    gather(0)
    gather(1)
    update(CHUNKS[2:])
    to_plane(0, pieces[2])
    gather(2, crossed[0][-1])
    to_tables(0)
    to_tables(1)
    to_cores(0)
    to_plane(1, *moved[0])
    multiply(0, 0)
    multiply(0, 1)
    to_tables(2, backs[0], moved[1][0])
    multiply(0, 2)
    multiply(0, 3)
    to_cores(1, backs[2])
    for q in range(4):
        multiply(1, q, 1 + q // 3)
    count = len(jobs)
    for j in range(count + 2):
        if j <= early and 1 <= j <= count:
            step_two(j - 1)
        if j < count:
            step_one(j)
        if j > early and j <= count:
            step_two(j - 1)
        if j >= 2:
            step_three(j - 2)
    result = [jnp.concatenate(result[:4], axis=1), jnp.concatenate(result[4:], axis=1)]
    decoded = jnp.concatenate(result, axis=0)
    return (*updated, decoded)


def solution(mesh):
    placed = (
        P(("fsdp", "tp"), None),
        P(("fsdp", "tp"), None),
        P(("fsdp", "tp"), None),
        P(("fsdp", "tp"), None),
        P("fsdp", "tp"),
    )
    return jax.shard_map(
        local,
        mesh=mesh,
        in_specs=placed,
        out_specs=(
            P(("fsdp", "tp"), None),
            P(("fsdp", "tp"), None),
            P(("fsdp", "tp"), None),
            P("fsdp", "tp"),
        ),
        check_vma=False,
    )
```

```python
import jax
import jax.numpy as jnp
from jax import lax
from jax.experimental import pallas as pl
from jax.experimental.pallas import tpu as pltpu
from jax.sharding import PartitionSpec as P

AXES = ("fsdp", "tp")
ROW_CHUNKS = 2
CHUNKS = ((0, 1), (1, 1), (2, 2))


def adam(where, chunks, args, previous):
    rows, cols = args[0].shape
    unit = cols // 16
    counts = [count for first, count in chunks]
    width = unit * sum(counts)
    step = max(s for s in range(16, 449, 16) if rows % s == 0)
    tiles = rows // step
    spread = cols // 4 // width
    start = chunks[0][0] * unit // width

    def kernel(where_ref, master_ref, one_ref, two_ref, grad_ref, *refs):
        outs = refs[-3 - len(chunks) :]
        grad = grad_ref[...].astype(jnp.float32)
        new_one = 0.9 * one_ref[...] + 0.1 * grad
        new_two = 0.95 * two_ref[...] + 0.05 * grad * grad
        new_master = master_ref[...] - 0.001 * new_one / (jnp.sqrt(new_two) + 1e-08)
        outs[0][...] = new_master
        outs[1][...] = new_one
        outs[2][...] = new_two
        at = 0
        for ref, count in zip(outs[3:], counts):
            for k in range(count):
                ref[k] = new_master[:, at : at + unit].astype(jnp.bfloat16)
                at += unit

    def at(i, w):
        return i % tiles, i // tiles * spread + start

    def piece_at(i, w):
        j = i // tiles
        return 0, i % tiles, 2 * ((j % 2) ^ w[1]) + ((j // 2) ^ w[0])

    block = pl.BlockSpec((step, width), at)
    full = jax.ShapeDtypeStruct((rows, cols), jnp.float32)
    size = 4 * rows * width
    out = pl.pallas_call(
        kernel,
        grid_spec=pltpu.PrefetchScalarGridSpec(
            num_scalar_prefetch=1,
            grid=(4 * tiles,),
            in_specs=[block] * 4 + [pl.BlockSpec(memory_space=pl.ANY)] * len(previous),
            out_specs=[block] * 3 + [pl.BlockSpec((count, step, unit), piece_at) for count in counts],
        ),
        out_shape=[full] * 3 + [jax.ShapeDtypeStruct((count, rows, 4 * unit), jnp.bfloat16) for count in counts],
        input_output_aliases={5 + i: i for i in range(len(previous))},
        compiler_params=pltpu.CompilerParams(vmem_limit_bytes=60 * 1024 * 1024),
        cost_estimate=pl.CostEstimate(flops=12 * size, bytes_accessed=28 * size, transcendentals=size),
        name="adam",
    )(where, *args, *previous)
    return out[:3], out[3:]


def pack(where, act, xs):
    rows, cols = act.shape
    run = cols // xs // 2
    part = rows // ROW_CHUNKS
    step = part // 2
    each = part // step

    def kernel(where_ref, act_ref, *out_refs):
        for y in range(2):
            for x in range(xs):
                for m in range(ROW_CHUNKS):

                    @pl.when((where_ref[0] == y) & (where_ref[2] == x) & (pl.program_id(0) // each == m))
                    def _():
                        for s in range(2):
                            for d in range(xs):
                                at = (2 * (x ^ d) + (y ^ s)) * run
                                out_refs[2 * m + s][:, d * run : (d + 1) * run] = act_ref[:, at : at + run]

    def rows_of(m):
        return lambda i: (jnp.clip(i - m * each, 0, each - 1), 0)

    out = pl.pallas_call(
        kernel,
        grid=(rows // step,),
        in_specs=[pl.BlockSpec(memory_space=pltpu.SMEM), pl.BlockSpec((step, cols), lambda i: (i, 0))],
        out_specs=[pl.BlockSpec((step, cols // 2), rows_of(m)) for m in range(ROW_CHUNKS) for s in range(2)],
        out_shape=[jax.ShapeDtypeStruct((part, cols // 2), act.dtype)] * (2 * ROW_CHUNKS),
        compiler_params=pltpu.CompilerParams(vmem_limit_bytes=60 * 1024 * 1024),
        cost_estimate=pl.CostEstimate(flops=0, bytes_accessed=4 * rows * cols, transcendentals=0),
        name="pack",
    )(where, act)
    return out[0::2], out[1::2]


def swap_if(flag, low, high):
    return jnp.where(flag, high, low), jnp.where(flag, low, high)


def after(value, *done):
    return lax.optimization_barrier((value, *done))[0] if done else value


def local(master, moment_one, moment_two, gradient, hidden_act):
    fsdp, tp = lax.axis_size("fsdp"), lax.axis_size("tp")
    xs = fsdp // tp
    f, t = lax.axis_index("fsdp"), lax.axis_index("tp")
    z, x, y, c = f // xs, f % xs, t // 2, t % 2
    where = jnp.stack([y, c, x]).astype(jnp.int32)

    def permute(value, to):
        pairs = []
        for zi in range(tp):
            for xi in range(xs):
                for yi in range(2):
                    for ci in range(2):
                        zo, xo, yo, co = to(zi, xi, yi, ci)
                        pairs.append(((zi * xs + xi) * tp + 2 * yi + ci, (zo * xs + xo) * tp + 2 * yo + co))
        return lax.ppermute(value, AXES, pairs)

    rows = hidden_act.shape[0]
    part = rows // ROW_CHUNKS
    own, other = pack(where, hidden_act, xs)

    args = (master, moment_one, moment_two, gradient)
    updated, pieces = [], []

    def update(chunks, *done):
        new, weights = adam(after(where, *done), chunks, args, updated)
        updated[:] = new
        pieces.extend(weights)

    flip = (c ^ (z % 2)) != 0
    crossed, tables = [], []
    theirs, pairs, moved, acts = [], [], [], []
    jobs, sends, backs = [], [], []
    nears, fars, halfway, leaving, result = [], [], [], [], []

    def cross(m, *done):
        theirs.append(permute(after(other[m], *done), lambda z, x, y, c: (z, x, 1 - y, c)))

    def to_plane(m, *done):
        pair = after(swap_if(((z // 2) ^ y) != 0, own[m], theirs[m]), *done)
        pairs.append(pair)
        moved.append(
            [permute(data, lambda z, x, y, c: (2 * ((z // 2) ^ a) + c, x, y, z % 2)) for a, data in enumerate(pair)]
        )

    def to_cores(m, *done):
        got = after(moved[m], *done)
        acts.append(got + [permute(data, lambda z, x, y, c: (z, x, y, 1 - c)) for data in got])

    def gather(q, *done):
        piece = after(pieces[q], *done)
        crossed.append([piece] + [permute(piece, lambda z, x, y, c: (z, x ^ d, y, c)) for d in range(1, xs)])

    def to_tables(q, *done):
        parts = after(crossed[q], *done)
        half = parts[0].shape[2] // 2
        for k in range(parts[0].shape[0]):
            near = jnp.stack([p[k, :, :half] for p in parts])
            far = jnp.stack([p[k, :, half:] for p in parts])
            far = permute(far, lambda z, x, y, c: (z, x, y, 1 - c))
            tables.append(jnp.stack(swap_if(c != 0, near, far), axis=1).reshape(-1, half))

    early = 5

    def multiply(m, q, pieces=1):
        half = tables[q].shape[1] // 2
        totals = [jnp.dot(a, tables[q], preferred_element_type=jnp.float32) for a in acts[m]]
        width = half // pieces
        for at in range(0, half, width):
            send = jnp.stack([total[:, half + at : half + at + width].astype(jnp.bfloat16) for total in totals])
            send = after(send, *sends[-1:], *backs[-2:-1])
            sends.append(send)
            backs.append(permute(send, lambda z, x, y, c: (z, x, 1 - y, c)))
            jobs.append([total[:, at : at + width] for total in totals])

    def step_one(j):
        done = leaving[j - 1 : j] if j <= early else leaving[j - 2 : j - 1]
        back = after(backs[j], *done)
        totals = [total + b for total, b in zip(jobs[j], back)]
        count = len(totals) // 2
        near, far = zip(*[swap_if(flip, own, sibling) for own, sibling in zip(totals[:count], totals[count:])])
        near, far = [jnp.concatenate(v, axis=0) if count > 1 else v[0] for v in (near, far)]
        nears.append(near)
        fars.append(far.astype(jnp.bfloat16))
        halfway.append(permute(fars[j], lambda z, x, y, c: (z ^ 1, x, y, c)))

    def step_two(j):
        back = after(halfway[j], *sends[j + 3 : j + 4])
        total = nears[j] + back
        leaving.append(total[part:].astype(jnp.bfloat16))
        nears[j] = total[:part]
        halfway[j] = permute(leaving[j], lambda z, x, y, c: (z ^ 2, x, y, c))

    def step_three(j):
        result.append((nears[j] + halfway[j]).astype(jnp.bfloat16))

    update(CHUNKS[:2], own[0])
    cross(0)
    cross(1)
    gather(0)
    gather(1)
    update(CHUNKS[2:])
    to_plane(0, pieces[2])
    gather(2, crossed[0][-1])
    to_tables(0)
    to_tables(1)
    to_cores(0)
    to_plane(1, *moved[0])
    multiply(0, 0)
    multiply(0, 1)
    to_tables(2, backs[0], moved[1][0])
    multiply(0, 2)
    multiply(0, 3)
    to_cores(1, backs[2])
    for q in range(4):
        multiply(1, q, 1 + q // 3)
    count = len(jobs)
    for j in range(count + 2):
        if j <= early and 1 <= j <= count:
            step_two(j - 1)
        if j < count:
            step_one(j)
        if j > early and j <= count:
            step_two(j - 1)
        if j >= 2:
            step_three(j - 2)
    result = [jnp.concatenate(result[:4], axis=1), jnp.concatenate(result[4:], axis=1)]
    decoded = jnp.concatenate(result, axis=0)
    return (*updated, decoded)


def solution(mesh):
    placed = (
        P(("fsdp", "tp"), None),
        P(("fsdp", "tp"), None),
        P(("fsdp", "tp"), None),
        P(("fsdp", "tp"), None),
        P("fsdp", "tp"),
    )
    return jax.shard_map(
        local,
        mesh=mesh,
        in_specs=placed,
        out_specs=(
            P(("fsdp", "tp"), None),
            P(("fsdp", "tp"), None),
            P(("fsdp", "tp"), None),
            P("fsdp", "tp"),
        ),
        check_vma=False,
    )
```

```python
import jax
import jax.numpy as jnp
from jax import lax
from jax.experimental import pallas as pl
from jax.experimental.pallas import tpu as pltpu
from jax.sharding import PartitionSpec as P

AXES = ("fsdp", "tp")
ROW_CHUNKS = 2
CHUNKS = ((0, 1), (1, 1), (2, 2))


def adam(where, chunks, args, previous):
    rows, cols = args[0].shape
    unit = cols // 16
    counts = [count for first, count in chunks]
    width = unit * sum(counts)
    step = max(s for s in range(16, 449, 16) if rows % s == 0)
    tiles = rows // step
    spread = cols // 4 // width
    start = chunks[0][0] * unit // width

    def kernel(where_ref, master_ref, one_ref, two_ref, grad_ref, *refs):
        outs = refs[-3 - len(chunks) :]
        grad = grad_ref[...].astype(jnp.float32)
        new_one = 0.9 * one_ref[...] + 0.1 * grad
        new_two = 0.95 * two_ref[...] + 0.05 * grad * grad
        new_master = master_ref[...] - 0.001 * new_one / (jnp.sqrt(new_two) + 1e-08)
        outs[0][...] = new_master
        outs[1][...] = new_one
        outs[2][...] = new_two
        at = 0
        for ref, count in zip(outs[3:], counts):
            for k in range(count):
                ref[k] = new_master[:, at : at + unit].astype(jnp.bfloat16)
                at += unit

    def at(i, w):
        return i % tiles, i // tiles * spread + start

    def piece_at(i, w):
        j = i // tiles
        return 0, i % tiles, 2 * ((j % 2) ^ w[1]) + ((j // 2) ^ w[0])

    block = pl.BlockSpec((step, width), at)
    full = jax.ShapeDtypeStruct((rows, cols), jnp.float32)
    size = 4 * rows * width
    out = pl.pallas_call(
        kernel,
        grid_spec=pltpu.PrefetchScalarGridSpec(
            num_scalar_prefetch=1,
            grid=(4 * tiles,),
            in_specs=[block] * 4 + [pl.BlockSpec(memory_space=pl.ANY)] * len(previous),
            out_specs=[block] * 3 + [pl.BlockSpec((count, step, unit), piece_at) for count in counts],
        ),
        out_shape=[full] * 3 + [jax.ShapeDtypeStruct((count, rows, 4 * unit), jnp.bfloat16) for count in counts],
        input_output_aliases={5 + i: i for i in range(len(previous))},
        compiler_params=pltpu.CompilerParams(vmem_limit_bytes=60 * 1024 * 1024),
        cost_estimate=pl.CostEstimate(flops=12 * size, bytes_accessed=28 * size, transcendentals=size),
        name="adam",
    )(where, *args, *previous)
    return out[:3], out[3:]


def pack(where, act, xs, m):
    rows, cols = act.shape
    run = cols // xs // 2
    part = rows // ROW_CHUNKS

    def kernel(where_ref, act_ref, *out_refs):
        for y in range(2):
            for x in range(xs):

                @pl.when((where_ref[0] == y) & (where_ref[2] == x))
                def _():
                    for s in range(2):
                        for d in range(xs):
                            at = (2 * (x ^ d) + (y ^ s)) * run
                            out_refs[s][:, d * run : (d + 1) * run] = act_ref[:, at : at + run]

    whole = pl.BlockSpec((part, cols // 2), lambda i: (0, 0))
    return pl.pallas_call(
        kernel,
        grid=(1,),
        in_specs=[pl.BlockSpec(memory_space=pltpu.SMEM), pl.BlockSpec((part, cols), lambda i: (m, 0))],
        out_specs=[whole] * 2,
        out_shape=[jax.ShapeDtypeStruct((part, cols // 2), act.dtype)] * 2,
        compiler_params=pltpu.CompilerParams(vmem_limit_bytes=60 * 1024 * 1024),
        cost_estimate=pl.CostEstimate(flops=0, bytes_accessed=4 * part * cols, transcendentals=0),
        name="pack",
    )(where, act)


def swap_if(flag, low, high):
    return jnp.where(flag, high, low), jnp.where(flag, low, high)


def after(value, *done):
    return lax.optimization_barrier((value, *done))[0] if done else value


def local(master, moment_one, moment_two, gradient, hidden_act):
    fsdp, tp = lax.axis_size("fsdp"), lax.axis_size("tp")
    xs = fsdp // tp
    f, t = lax.axis_index("fsdp"), lax.axis_index("tp")
    z, x, y, c = f // xs, f % xs, t // 2, t % 2
    where = jnp.stack([y, c, x]).astype(jnp.int32)

    def permute(value, to):
        pairs = []
        for zi in range(tp):
            for xi in range(xs):
                for yi in range(2):
                    for ci in range(2):
                        zo, xo, yo, co = to(zi, xi, yi, ci)
                        pairs.append(((zi * xs + xi) * tp + 2 * yi + ci, (zo * xs + xo) * tp + 2 * yo + co))
        return lax.ppermute(value, AXES, pairs)

    rows = hidden_act.shape[0]
    part = rows // ROW_CHUNKS
    own, other = [], []

    args = (master, moment_one, moment_two, gradient)
    updated, pieces = [], []

    def update(chunks, *done):
        new, weights = adam(after(where, *done), chunks, args, updated)
        updated[:] = new
        pieces.extend(weights)

    flip = (c ^ (z % 2)) != 0
    crossed, tables = [], []
    theirs, pairs, moved, acts = [], [], [], []
    jobs, sends, backs = [], [], []
    nears, fars, halfway, leaving, result = [], [], [], [], []

    def cross(m, *done):
        theirs.append(permute(after(other[m], *done), lambda z, x, y, c: (z, x, 1 - y, c)))

    def to_plane(m, *done):
        pair = after(swap_if(((z // 2) ^ y) != 0, own[m], theirs[m]), *done)
        pairs.append(pair)
        moved.append(
            [permute(data, lambda z, x, y, c: (2 * ((z // 2) ^ a) + c, x, y, z % 2)) for a, data in enumerate(pair)]
        )

    def to_cores(m, *done):
        got = after(moved[m], *done)
        acts.append(got + [permute(data, lambda z, x, y, c: (z, x, y, 1 - c)) for data in got])

    def gather(q, *done):
        piece = after(pieces[q], *done)
        crossed.append([piece] + [permute(piece, lambda z, x, y, c: (z, x ^ d, y, c)) for d in range(1, xs)])

    def to_tables(q, *done):
        parts = after(crossed[q], *done)
        half = parts[0].shape[2] // 2
        for k in range(parts[0].shape[0]):
            near = jnp.stack([p[k, :, :half] for p in parts])
            far = jnp.stack([p[k, :, half:] for p in parts])
            far = permute(far, lambda z, x, y, c: (z, x, y, 1 - c))
            tables.append(jnp.stack(swap_if(c != 0, near, far), axis=1).reshape(-1, half))

    early = 5

    def multiply(m, q, pieces=1):
        half = tables[q].shape[1] // 2
        totals = [jnp.dot(a, tables[q], preferred_element_type=jnp.float32) for a in acts[m]]
        width = half // pieces
        for at in range(0, half, width):
            send = jnp.stack([total[:, half + at : half + at + width].astype(jnp.bfloat16) for total in totals])
            send = after(send, *sends[-1:], *backs[-2:-1])
            sends.append(send)
            backs.append(permute(send, lambda z, x, y, c: (z, x, 1 - y, c)))
            jobs.append([total[:, at : at + width] for total in totals])

    def step_one(j):
        done = leaving[j - 1 : j] if j <= early else leaving[j - 2 : j - 1]
        back = after(backs[j], *done)
        totals = [total + b for total, b in zip(jobs[j], back)]
        count = len(totals) // 2
        near, far = zip(*[swap_if(flip, own, sibling) for own, sibling in zip(totals[:count], totals[count:])])
        near, far = [jnp.concatenate(v, axis=0) if count > 1 else v[0] for v in (near, far)]
        nears.append(near)
        fars.append(far.astype(jnp.bfloat16))
        halfway.append(permute(fars[j], lambda z, x, y, c: (z ^ 1, x, y, c)))

    def step_two(j):
        back = after(halfway[j], *sends[j + 3 : j + 4])
        total = nears[j] + back
        leaving.append(total[part:].astype(jnp.bfloat16))
        nears[j] = total[:part]
        halfway[j] = permute(leaving[j], lambda z, x, y, c: (z ^ 2, x, y, c))

    def step_three(j):
        result.append((nears[j] + halfway[j]).astype(jnp.bfloat16))

    def fill(m, *done):
        for parts, value in zip((own, other), pack(after(where, *done), hidden_act, xs, m)):
            parts.append(value)

    fill(0)
    update(CHUNKS[:2], own[0])
    cross(0)
    gather(0)
    gather(1)
    update(CHUNKS[2:])
    to_plane(0, pieces[2])
    fill(1, *pairs[0])
    cross(1)
    gather(2, crossed[0][-1])
    to_tables(0)
    to_tables(1)
    to_cores(0)
    to_plane(1, *moved[0])
    multiply(0, 0)
    multiply(0, 1)
    to_tables(2, backs[0], moved[1][0])
    multiply(0, 2)
    multiply(0, 3)
    to_cores(1, backs[2])
    for q in range(4):
        multiply(1, q, 1 + q // 3)
    count = len(jobs)
    for j in range(count + 2):
        if j <= early and 1 <= j <= count:
            step_two(j - 1)
        if j < count:
            step_one(j)
        if j > early and j <= count:
            step_two(j - 1)
        if j >= 2:
            step_three(j - 2)
    result = [jnp.concatenate(result[:4], axis=1), jnp.concatenate(result[4:], axis=1)]
    decoded = jnp.concatenate(result, axis=0)
    return (*updated, decoded)


def solution(mesh):
    placed = (
        P(("fsdp", "tp"), None),
        P(("fsdp", "tp"), None),
        P(("fsdp", "tp"), None),
        P(("fsdp", "tp"), None),
        P("fsdp", "tp"),
    )
    return jax.shard_map(
        local,
        mesh=mesh,
        in_specs=placed,
        out_specs=(
            P(("fsdp", "tp"), None),
            P(("fsdp", "tp"), None),
            P(("fsdp", "tp"), None),
            P("fsdp", "tp"),
        ),
        check_vma=False,
    )
```
